256 devices in a mesh: dom: 256 (over z, x, y, core).
Axes of the slice: x: 4, y: 4, z: 8, core: 2. Of those that a mesh axis runs over, the one named last changes fastest.
Arguments:
- coef_init: float32 [1024, 128], P('dom'), may hold values from -6 to 6
- basis: bfloat16 [393216, 1024], P('dom'), may hold values from -0.75 to 0.75
- basis_scale: float32 [3072], P('dom'), may hold values from 0.5 to 2
- ext_force: float32 [393216, 128], P('dom'), may hold values from -6 to 6
- precond: float32 [1024], P('dom'), may hold values from 0.5 to 6, as said below
- connectivity: int32 [115200, 8], P('dom'), may hold values from 0 to 767, as said below
- halo_nodes: int32 [65536], P('dom'), may hold values from 0 to 511, as said below
- plastic: int32 [115200], P('dom'), may hold values 0 or 1
Outputs:
- coef_final: float32 [1024, 128], P('dom')
- nodal_residual: float32 [393216, 128], P('dom')
The draws below stay inside these ranges and needn't reach their ends.
Inputs may be any that keep to these rules, and one draw needn't show every extreme that they name: `connectivity`: each part is a structured block of 16 x 16 x 2 nodes, numbered in a part-specific order; each row lists an element's 8 corners in corner-bit order (bit 0 along x, bit 1 along y, bit 2 along z). Entries below 512 are the part's own nodes; an entry 512 + h names the node listed h-th in the next part's halo_nodes (the next part's first z layer). `halo_nodes`: the entries of one part are its own local node numbers of its first z layer, in grid order with x fastest, all distinct. `precond`: Positive.
All inputs are finite; a program needn't handle non-finite values. No bound on the sum of `plastic` on one device may be relied on, other than what follows from the above.
Results may differ from the reference program's by a relative error of at most 0.0087.
Values may be sent and summed in bfloat16 or wider, within the bound.
A program may use at most 64 MiB of HBM per device.

```python
import math
import jax
import jax.numpy as jnp
from jax import lax

R = 1024
C = 128
GX = 16
GY = 16
GZ = 2
TILE = 128
ITERS = 2
NODE_DEV = 512
ELEM_DEV = 450
HALO = 256
NODES = 131072
ROWS = 393216
ELEMS = 115200
N_DOM = 256


def part_numbering(subkey):
    count = GX * GY * GZ
    scores = jax.random.randint(subkey, (count,), 0, 2 ** 18, jnp.int32) * count + jnp.arange(count, dtype=jnp.int32)
    scores = scores.at[0].set(-1).at[1].set(2 ** 30)
    order = jnp.argsort(scores, stable=True).astype(jnp.int32)
    return jnp.argsort(order, stable=True).astype(jnp.int32)


def mesh_numbering(key):
    node_keys = jax.random.split(jax.random.fold_in(key, 7), N_DOM)
    node_perm = jax.vmap(part_numbering)(node_keys)
    elem_keys = jax.random.split(jax.random.fold_in(key, 11), N_DOM)
    elem_perm = jax.vmap(lambda subkey: jax.random.permutation(subkey, (GX - 1) * (GY - 1) * GZ))(elem_keys)
    return (node_perm.astype(jnp.int32), elem_perm.astype(jnp.int32))


def draw_halo_nodes(key, part):
    node_perm, elem_perm = mesh_numbering(key)
    return node_perm[:, :GX * GY].reshape(-1).astype(jnp.int32)


def draw_connectivity(key, part):
    node_perm, elem_perm = mesh_numbering(key)
    element = jnp.arange((GX - 1) * (GY - 1) * GZ, dtype=jnp.int32)
    cell_x = element % (GX - 1)
    cell_y = element // (GX - 1) % (GY - 1)
    cell_z = element // ((GX - 1) * (GY - 1))
    corner = jnp.arange(8, dtype=jnp.int32)
    point_x = cell_x[:, None] + (corner & 1)[None, :]
    point_y = cell_y[:, None] + (corner >> 1 & 1)[None, :]
    point_z = cell_z[:, None] + (corner >> 2 & 1)[None, :]
    grid_point = jnp.minimum(point_z, GZ - 1) * GX * GY + point_y * GX + point_x
    own_index = node_perm[:, grid_point]
    halo_index = GX * GY * GZ + point_y * GX + point_x
    local_index = jnp.where(point_z[None] < GZ, own_index, halo_index[None])
    shuffled = jnp.take_along_axis(local_index, elem_perm[:, :, None], axis=1)
    return shuffled.reshape(-1, 8).astype(jnp.int32)


def draw_precond(key, part):
    position = jnp.arange(R, dtype=jnp.float32) / R
    factor = jnp.exp(jax.random.uniform(key, (R,), jnp.float32, -0.35, 0.35))
    rising = 1.0 + 2.0 * position
    return (rising * factor).astype(jnp.float32)


def plant(values, rng, low, top_value):
    extent = values.shape
    spot = [jax.random.randint(jax.random.fold_in(rng, axis), (), 0, extent[axis]) for axis in range(len(extent))]
    values = values.at[tuple(spot)].set(low)
    longest = extent.index(max(extent))
    spot[longest] = (spot[longest] + 1) % extent[longest]
    return values.at[tuple(spot)].set(top_value)


def strengthened(drawn, own_key, source, target, shards_of, factor):
    owner, partner = [(jnp.arange(drawn.shape[dim]) // (drawn.shape[dim] // shards_of)).reshape([-1 if axis == dim else 1 for axis in range(drawn.ndim)]) for dim in (source, target)]
    chosen = jax.random.permutation(own_key, shards_of)[partner]
    strong = (owner == chosen) | (owner == (partner + shards_of // 2) % shards_of)
    return jnp.where(strong, factor * drawn, drawn)


def steps_of(own_key, extent, cuts, low, largest):
    gain, own = 1.0, jax.random.fold_in(own_key, 6)
    for dim, blocks in cuts:
        heights = jnp.exp(jax.random.uniform(jax.random.fold_in(own, dim), (blocks,), jnp.float32, low / len(cuts), largest / len(cuts)))
        gain = gain * jnp.repeat(heights, extent[dim] // blocks).reshape([-1 if axis == dim else 1 for axis in range(len(extent))])
    return gain


def centred(stream_key, extent, deviation, bound, shards=(), held_as=jnp.bfloat16):
    entries = jax.random.normal(stream_key, extent, jnp.float32) * deviation
    if len(shards) > 0:
        entries = steps_of(stream_key, extent, shards, -0.22, 0.18) * entries
    return jnp.clip(entries, min=-bound, max=bound).astype(held_as)


def noise_with(rng, shape, deviation, bound, cuts, heavy, kind=jnp.bfloat16):
    values = deviation * jax.random.normal(rng, shape, jnp.float32)
    if cuts:
        values = values * steps_of(rng, shape, cuts, -0.22, 0.18)
    return jnp.clip(strengthened(values, jax.random.fold_in(rng, 3), *heavy), -bound, bound).astype(kind)


def setup_inputs(seed: int = 0) -> dict:
    key_list = jax.random.split(jax.random.key(seed), 9)
    return {
        "coef_init": centred(key_list[0], (R, C), 1.0, 6.0, ((0, 256),), jnp.float32),
        "basis": noise_with(key_list[1], (ROWS, R), R ** -0.5, 0.75, ((0, 256),), (0, 1, 256, 6.0)),
        "basis_scale": jnp.clip(jnp.exp(math.log(2.0) - 1.3862944 * jax.random.uniform(key_list[2], (ROWS // TILE,), jnp.float32) ** steps_of(key_list[2], (ROWS // TILE,), ((0, 256),), -0.2, 0.2)), 0.5, 2.0),
        "ext_force": centred(key_list[3], (ROWS, C), 1.0, 6.0, ((0, 256),), jnp.float32),
        "precond": draw_precond(jax.random.fold_in(key_list[8], 71), 0),
        "connectivity": draw_connectivity(jax.random.fold_in(key_list[8], 71), 0),
        "halo_nodes": draw_halo_nodes(jax.random.fold_in(key_list[8], 71), 0),
        "plastic": plant((jax.random.randint(key_list[7], (ELEMS,), 0, 2) < 1).astype(jnp.int32), jax.random.fold_in(key_list[7], 1), 0, 1),
    }


STEP_SIZE = 0.5
SHEAR_MODULUS = 1.0
LAME_FIRST = 1.5
HARDENING = 0.5
YIELD_STRESS = 3.0
EPSILON = 1e-05

def corner_table():
    corner_bits = jnp.arange(8)[:, None] >> jnp.arange(3)[None, :] & 1
    return (2.0 * corner_bits.astype(jnp.float32) - 1.0) / 4.0

def element_forces(corner_disp, flags, corners):
    gradient = jnp.einsum('eaic,aj->eijc', corner_disp, corners, precision=lax.Precision.HIGHEST)
    strain = 0.5 * (gradient + jnp.swapaxes(gradient, 1, 2))
    volumetric = strain[:, 0, 0] + strain[:, 1, 1] + strain[:, 2, 2]
    identity = jnp.eye(3, dtype=jnp.float32)[None, :, :, None]
    shear_part = 2.0 * SHEAR_MODULUS * (strain - volumetric[:, None, None] / 3.0 * identity)
    magnitude = jnp.sqrt(lax.optimization_barrier(jnp.sum(shear_part * shear_part, axis=(1, 2))))
    total_modulus = 2.0 * SHEAR_MODULUS + HARDENING
    plastic_factor = HARDENING / total_modulus + 2.0 * SHEAR_MODULUS * YIELD_STRESS / (total_modulus * jnp.maximum(magnitude, YIELD_STRESS))
    factor = jnp.where(flags[:, None] == 1, plastic_factor, jnp.ones_like(plastic_factor))
    stress = LAME_FIRST * volumetric[:, None, None] * identity + factor[:, None, None] * shear_part
    return jnp.einsum('eijc,aj->eaic', stress, corners, precision=lax.Precision.HIGHEST)

def apply_scale(values, scales):
    return (values.reshape(scales.shape[0], -1, values.shape[-1]) * scales[:, None, None]).reshape(values.shape)

def reference(coef_init, basis, basis_scale, ext_force, precond, connectivity, halo_nodes, plastic):
    corners = corner_table()
    cases = coef_init.shape[1]
    element_device = (jnp.arange(ELEMS) // ELEM_DEV).astype(jnp.int32)[:, None]
    halo_padded = jnp.concatenate([halo_nodes, jnp.zeros((HALO,), jnp.int32)])
    halo_slot = jnp.clip(connectivity - NODE_DEV, 0, HALO - 1).astype(jnp.int32)
    neighbour = element_device + 1
    halo_target = neighbour * NODE_DEV + halo_padded[(neighbour * HALO + halo_slot).astype(jnp.int32)]
    global_index = jnp.where(connectivity < NODE_DEV, element_device * NODE_DEV + connectivity, halo_target).astype(jnp.int32)
    blocks = (global_index.reshape(N_DOM, ELEM_DEV, 8), plastic.reshape(N_DOM, ELEM_DEV))
    coefficients = coef_init
    nodal_residual = ext_force
    for sweep in range(ITERS):
        coef_low = coefficients.astype(jnp.bfloat16)
        displacement = apply_scale(jnp.dot(basis, coef_low, preferred_element_type=jnp.float32), basis_scale)
        nodes = jnp.concatenate([displacement.reshape(NODES, 3, cases), jnp.zeros((NODE_DEV, 3, cases), jnp.float32)])

        def accumulate(internal, inputs):
            block_index, flags = inputs
            corner_force = element_forces(nodes[block_index], flags, corners)
            return (internal.at[block_index.reshape(-1)].add(corner_force.reshape(-1, 3, cases)), None)
        internal, unused = lax.scan(accumulate, jnp.zeros((NODES + NODE_DEV, 3, cases), jnp.float32), blocks)
        nodal_residual = ext_force - internal[:NODES].reshape(ROWS, cases)
        scaled = apply_scale(nodal_residual, basis_scale).astype(jnp.bfloat16)
        reduced = lax.dot_general(basis, scaled, (((0,), (0,)), ((), ())), preferred_element_type=jnp.float32)
        update = precond[:, None] * reduced
        root_mean = jnp.sqrt(lax.optimization_barrier(jnp.mean(update * update, axis=0)) + EPSILON)
        coefficients = coefficients + STEP_SIZE * update / root_mean
    return (coefficients, nodal_residual)
```

```python
import functools

import jax
import jax.numpy as jnp
from jax import lax
from jax.experimental import pallas as pl
from jax.experimental.pallas import tpu as pltpu
from jax.sharding import PartitionSpec as P

MESH = pl.DeviceIdType.MESH
F32, BF16 = jnp.float32, jnp.bfloat16

R = 1024
C = 128
ROWS = 1536
LAYER = 256
ELEMS = 450
NDEV = 256
NZ = 8
NQ = 32
BLOCK = 32
CHUNK = 32
STEP_SIZE = 0.5
EPSILON = 1e-05


def dot(a, b):
    return jnp.dot(a, b, preferred_element_type=F32)


def split3(x):
    hi = x.astype(BF16)
    rest = x - hi.astype(F32)
    mid = rest.astype(BF16)
    low = (rest - mid.astype(F32)).astype(BF16)
    return jnp.concatenate([hi, mid, low], axis=1)


def peak(x):
    x = jnp.abs(x)
    for _ in range(x.ndim - 2):
        x = jnp.max(x, axis=0)
    return jnp.maximum(jnp.max(x, axis=0, keepdims=True), 1e-30)


def to_steps(x, top):
    return jnp.round(x * (32767.0 / top)).astype(jnp.int32).astype(jnp.int16)


def from_steps(steps, top):
    return steps.astype(jnp.int32).astype(F32) * (top * (1.0 / 32767.0))


def iota(shape, axis):
    return lax.broadcasted_iota(jnp.int32, shape, axis)


def swap4(x):
    return pltpu.roll(x, 4, x.ndim - 2)


def low_half(shape):
    return iota(shape, len(shape) - 2) % 8 < 4


def kernel(
    coef_ref, scale_ref, precond_ref, conn_ref, halo_ref, plastic_ref, basis_hbm, ext_hbm,
    final_ref, resid_hbm,
    basis, ext, sel, grid_basis, grid_basis_t, scale, grid_ext, resid, out_local, disp, weight, conn,
    tiles, block_init, precond32, gathered, gathered0, coef_low, scaled,
    halo_send, halo_recv, weight_send, weight_recv,
    reduced, part_send, part_recv, zsum_recv, update_recv, square_recv, own_update,
    rest, halo_top, part_top, zsum_top, update_top,
    local_sem, tile_sem, block_sem, halo_sem, weight_sem, part_sem, zsum_sem, update_sem, square_sem, rest_sem,
):
    me = lax.axis_index("dom")
    z, q = me // NQ, me % NQ
    nxt, prv = (me + 1) % NDEV, (me + NDEV - 1) % NDEV

    load_basis = pltpu.make_async_copy(basis_hbm, basis, local_sem.at[0])
    load_ext = pltpu.make_async_copy(ext_hbm, ext, local_sem.at[1])
    load_basis.start()
    load_ext.start()

    def in_plane(j):
        return z * NQ + (q + j) % NQ

    def in_column(j):
        return ((z + j) % NZ) * NQ + q

    barrier = pltpu.get_barrier_semaphore()

    def greet_plane(j, c):
        pl.semaphore_signal(barrier, inc=1, device_id=(in_plane(j),), device_id_type=MESH)
        return c

    def greet_column(j, c):
        pl.semaphore_signal(barrier, inc=1, device_id=(in_column(j),), device_id_type=MESH)
        return c

    lax.fori_loop(1, NQ, greet_plane, 0)
    lax.fori_loop(1, NZ, greet_column, 0)
    pl.semaphore_signal(barrier, inc=1, device_id=(nxt,), device_id_type=MESH)
    pl.semaphore_signal(barrier, inc=1, device_id=(prv,), device_id_type=MESH)

    tiles[z, 0:4, :] = coef_ref[...]
    row4 = iota((4, C), 0)
    pre = jnp.zeros((4, C), F32)
    for k in range(4):
        pre = jnp.where(row4 == k, precond_ref[k], pre)
    tiles[z, 4:8, :] = pre

    pl.semaphore_wait(barrier, NQ - 1 + NZ - 1 + 2)

    def send_column(src, buf, sems):
        def body(j, c):
            pltpu.make_async_remote_copy(
                src, buf.at[z], sems.at[0], sems.at[1], device_id=(in_column(j),), device_id_type=MESH
            ).start()
            return c

        lax.fori_loop(1, NZ, body, 0)

    def send_plane(src_of, buf, sems):
        def body(j, c):
            pltpu.make_async_remote_copy(
                src_of((q + j) % NQ), buf.at[q], sems.at[0], sems.at[1], device_id=(in_plane(j),), device_id_type=MESH
            ).start()
            return c

        lax.fori_loop(1, NQ, body, 0)

    def wait_for(buf, count, sem):
        part = buf.at[pl.ds(0, count)]
        pltpu.make_async_copy(part, part, sem).wait()

    send_column(tiles.at[z], tiles, tile_sem)

    conn[...] = jnp.full(conn.shape, -1.0, F32)
    conn[0:8, 0:ELEMS] = conn_ref[...].astype(F32)
    conn[8:9, 0:ELEMS] = plastic_ref[...].astype(F32)
    halo_row = halo_ref[...].astype(F32)
    eye = iota((LAYER, LAYER), 0) == iota((LAYER, LAYER), 1)
    node0 = jnp.sum(jnp.where(eye, halo_row, 0.0), axis=1, keepdims=True)
    place = iota((LAYER, 512), 0).astype(F32) + 512.0
    found = jnp.full((LAYER, 512), -1.0, F32)
    for a in range(4):
        found = jnp.maximum(found, jnp.where(conn[4 + a : 5 + a, :] == place, conn[a : a + 1, :], -1.0))
    node1 = jnp.max(found, axis=1, keepdims=True)
    flags = conn[8:9, :]
    flag1 = jnp.sum(jnp.where(conn[0:1, :] == node0, flags, 0.0), axis=1, keepdims=True)
    flag2 = jnp.sum(jnp.where(conn[4:5, :] == place, flags, 0.0), axis=1, keepdims=True)
    cell = iota((LAYER, C), 0)
    valid = (cell % 16 < 15) & (cell // 16 < 15)
    weight[1] = jnp.where(valid, 1.0 + flag1, 0.0)
    weight[2] = jnp.where(valid, 1.0 + flag2, 0.0)
    weight_send[...] = weight[2].astype(BF16)
    to_next = pltpu.make_async_remote_copy(
        weight_send, weight_recv, weight_sem.at[0], weight_sem.at[1], device_id=(nxt,), device_id_type=MESH
    )
    to_next.start()

    column = iota((LAYER, ROWS), 1)
    for layer, node in enumerate((node0, node1)):
        node3 = node.astype(jnp.int32) * 3
        for i in range(3):
            at = (layer * 3 + i) * LAYER
            sel[at : at + LAYER, :] = jnp.where(column == node3 + i, 1.0, 0.0).astype(BF16)
            tile = jnp.broadcast_to((node3 + i) >> 7, (LAYER, C))
            value = jnp.zeros((LAYER, C), F32)
            for t in range(12):
                value = jnp.where(tile == t, scale_ref[t], value)
            scale[at : at + LAYER, :] = value

    wait_for(tiles, NZ - 1, tile_sem.at[1])
    low = low_half((8, C))
    for j in range(4):
        a, b = tiles[2 * j], tiles[2 * j + 1]
        block_init[8 * j : 8 * j + 8, :] = jnp.where(low, a, swap4(b))
        precond32[8 * j : 8 * j + 8, :] = jnp.where(low, swap4(a), b)
    first = block_init[...].astype(BF16)
    gathered[q] = first
    send_plane(lambda _: gathered.at[q], gathered, block_sem)
    rest[q] = (block_init[...] - first.astype(F32)).astype(BF16)
    send_plane(lambda _: rest.at[q], rest, rest_sem)

    load_basis.wait()

    def permute(c, carry):
        rows = pl.ds(pl.multiple_of(c * LAYER, LAYER), LAYER)
        grid_basis[rows, :] = dot(sel[rows, :], basis[...]).astype(BF16)
        return carry

    lax.fori_loop(0, 6, permute, 0)

    zero_rows = jnp.zeros((16, C), F32)
    for k in range(12):
        disp[k, LAYER : LAYER + 16, :] = zero_rows
    for k in range(6):
        resid[k, LAYER : LAYER + 16, :] = zero_rows

    def place_rows(values):
        v = values.reshape(16, 2, 4, 8, C)
        first, second = v[:, 0], v[:, 1]
        mask = low_half((16, 4, 8, C))
        even = jnp.where(mask, first, swap4(second))
        odd = jnp.where(mask, swap4(first), second)
        for j in range(4):
            coef_low[256 * j : 256 * j + 128, :] = even[:, j].reshape(128, C).astype(BF16)
            coef_low[256 * j + 128 : 256 * j + 256, :] = odd[:, j].reshape(128, C).astype(BF16)

    wait_for(gathered, NQ - 1, block_sem.at[1])
    place_rows(gathered[...].astype(F32))

    def elements(k):
        def body(c, carry):
            at = pl.multiple_of(c * CHUNK, CHUNK)
            node_rows = pl.ds(at, CHUNK + 16)
            n = CHUNK + 16
            grad = []
            for i in range(3):
                under, over = disp[3 * k + i, node_rows, :], disp[3 * k + 3 + i, node_rows, :]
                under1, over1 = pltpu.roll(under, n - 1, 0), pltpu.roll(over, n - 1, 0)
                both, both1 = under + over, under1 + over1
                dx = both1 - both
                sx = both1 + both
                sz = (over1 + over) - (under1 + under)
                grad.append((dx[16:] + dx[:CHUNK], sx[16:] - sx[:CHUNK], sz[16:] + sz[:CHUNK]))
            w = weight[k, pl.ds(at, CHUNK), :]
            third = (grad[0][0] + grad[1][1] + grad[2][2]) * (1.0 / 6.0)
            sxx = grad[0][0] * 0.5 - third
            syy = grad[1][1] * 0.5 - third
            szz = grad[2][2] * 0.5 - third
            sxy = (grad[0][1] + grad[1][0]) * 0.25
            sxz = (grad[0][2] + grad[2][0]) * 0.25
            syz = (grad[1][2] + grad[2][1]) * 0.25
            mag2 = sxx * sxx + syy * syy + szz * szz + 2.0 * (sxy * sxy + sxz * sxz + syz * syz)
            plastic = 0.05 + 0.6 * lax.rsqrt(jnp.maximum(mag2, 9.0))
            factor = jnp.where(w > 1.5, plastic, jnp.where(w > 0.5, 0.25, 0.0))
            vol = jnp.where(w > 0.5, third * 0.5625, 0.0)
            stress = {
                (0, 0): vol + factor * sxx, (1, 1): vol + factor * syy, (2, 2): vol + factor * szz,
                (0, 1): factor * sxy, (0, 2): factor * sxz, (1, 2): factor * syz,
            }
            back = {ij: pltpu.roll(s, 1, 0) for ij, s in stress.items()}
            pad = jnp.zeros((16, C), F32)
            for i in range(3):
                ix, iy, iz = (0, i), (min(i, 1), max(i, 1)), (i, 2)
                dx = back[ix] - stress[ix]
                sy = back[iy] + stress[iy]
                sz = back[iz] + stress[iz]
                near, far = dx - sy, dx + sy
                if k >= 1:
                    rows = (3 * (k - 1) + i, node_rows, slice(None))
                    resid[rows] -= jnp.concatenate([near - sz, pad], 0) + jnp.concatenate([pad, far - sz], 0)
                if k <= 1:
                    rows = (3 * k + i, node_rows, slice(None))
                    resid[rows] -= jnp.concatenate([near + sz, pad], 0) + jnp.concatenate([pad, far + sz], 0)
            return carry

        lax.fori_loop(0, LAYER // CHUNK, body, 0)

    for sweep in range(2):
        def displace(c, carry):
            rows = pl.ds(pl.multiple_of(c * LAYER, LAYER), LAYER)
            u = dot(grid_basis[rows, :], coef_low[...]) * scale[rows, :]
            disp[c + 3, 0:LAYER, :] = u
            return carry

        copies = []
        for layer, (there, side) in enumerate(((prv, 1), (nxt, 0))):
            lax.fori_loop(3 * layer, 3 * layer + 3, displace, 0)
            u = disp[3 + 3 * layer : 6 + 3 * layer, 0:LAYER, :]
            top = peak(u)
            halo_top[sweep, layer] = top
            halo_send[sweep, layer] = to_steps(u, top)
            for src, dst, sem in (
                (halo_send.at[sweep, layer], halo_recv.at[sweep, side], 0),
                (halo_top.at[sweep, layer], halo_top.at[sweep, 2 + side], 1),
            ):
                copy = pltpu.make_async_remote_copy(
                    src, dst, halo_sem.at[sweep, layer, sem, 0], halo_sem.at[sweep, layer, sem, 1],
                    device_id=(there,), device_id_type=MESH,
                )
                copy.start()
                copies.append(copy)

        if sweep == 0:
            load_ext.wait()
            ext3 = split3(ext[...])

            def permute_ext(c, carry):
                rows = pl.ds(pl.multiple_of(c * LAYER, LAYER), LAYER)
                e = dot(sel[rows, :], ext3)
                grid_ext[c] = e[:, 0:C] + e[:, C : 2 * C] + e[:, 2 * C :]
                return carry

            lax.fori_loop(0, 6, permute_ext, 0)

            def turn(c, carry):
                rows = pl.ds(pl.multiple_of(c * LAYER, LAYER), LAYER)
                for b in range(4):
                    grid_basis_t[b * 256 : b * 256 + 256, rows] = grid_basis[rows, b * 256 : b * 256 + 256].T
                return carry

            lax.fori_loop(0, 6, turn, 0)
            to_next.wait()
            weight[0] = jnp.where(me > 0, weight_recv[...].astype(F32), 0.0)

        resid[:, 0:LAYER, :] = grid_ext[...]
        elements(1)
        for copy in copies:
            copy.wait()
        disp[0:3, 0:LAYER, :] = from_steps(halo_recv[sweep, 0], halo_top[sweep, 2][None])
        disp[9:12, 0:LAYER, :] = jnp.where(
            me < NDEV - 1, from_steps(halo_recv[sweep, 1], halo_top[sweep, 3][None]), 0.0
        )
        elements(0)
        elements(2)
        for k in range(6):
            rows = slice(k * LAYER, (k + 1) * LAYER)
            scaled[rows, :] = (resid[k, 0:LAYER, :] * scale[rows, :]).astype(BF16)

        def project(j, carry):
            rows = pl.ds(pl.multiple_of(j * 256, 256), 256)
            r = dot(grid_basis_t[rows, :], scaled[...]).reshape(2, 16, 8, C)
            even, odd = r[0], r[1]
            mask = low_half((16, 8, C))
            at = pl.ds(pl.multiple_of(j * 8, 8), 8)
            reduced[:, 0, at, :] = jnp.where(mask, even, swap4(odd))
            reduced[:, 1, at, :] = jnp.where(mask, swap4(even), odd)
            return carry

        lax.fori_loop(0, 4, project, 0)
        parts = reduced[...].reshape(NQ, BLOCK, C)
        top = peak(parts)
        part_top[sweep, q] = top
        send_plane(lambda _: part_top.at[sweep, q], part_top.at[sweep], part_sem.at[sweep, 1])
        part_send[sweep] = to_steps(parts, top[None])
        part_recv[sweep, q] = part_send[sweep, q]
        send_plane(lambda t: part_send.at[sweep, t], part_recv.at[sweep], part_sem.at[sweep, 0])

        if sweep == 1:
            out_local[...] = jnp.zeros_like(out_local)

            def restore(c, carry):
                rows = pl.ds(pl.multiple_of(c * LAYER, LAYER), LAYER)
                o = lax.dot_general(
                    sel[rows, :], split3(resid[c, 0:LAYER, :]), (((0,), (0,)), ((), ())), preferred_element_type=F32
                )
                out_local[...] += o[:, 0:C] + o[:, C : 2 * C] + o[:, 2 * C :]
                return carry

            lax.fori_loop(0, 6, restore, 0)
            store = pltpu.make_async_copy(out_local, resid_hbm, local_sem.at[2])
            store.start()

        wait_for(part_top.at[sweep], NQ - 1, part_sem.at[sweep, 1, 1])
        wait_for(part_recv.at[sweep], NQ - 1, part_sem.at[sweep, 0, 1])
        total = from_steps(part_recv[sweep, 0], part_top[sweep, 0])
        for t in range(1, NQ):
            total += from_steps(part_recv[sweep, t], part_top[sweep, t])
        top = peak(total)
        zsum_top[sweep, z] = top
        send_column(zsum_top.at[sweep, z], zsum_top.at[sweep], zsum_sem.at[sweep, 1])
        zsum_recv[sweep, z] = to_steps(total, top)
        send_column(zsum_recv.at[sweep, z], zsum_recv.at[sweep], zsum_sem.at[sweep, 0])
        wait_for(zsum_top.at[sweep], NZ - 1, zsum_sem.at[sweep, 1, 1])
        wait_for(zsum_recv.at[sweep], NZ - 1, zsum_sem.at[sweep, 0, 1])
        total = from_steps(zsum_recv[sweep, 0], zsum_top[sweep, 0])
        for t in range(1, NZ):
            total += from_steps(zsum_recv[sweep, t], zsum_top[sweep, t])
        update = total * precond32[...]

        if sweep == 0:
            own_update[...] = update
            top = peak(update)
            update_top[q] = top
            send_plane(lambda _: update_top.at[q], update_top, update_sem.at[1])
            update_recv[q] = to_steps(update, top)
            send_plane(lambda _: update_recv.at[q], update_recv, update_sem.at[0])
            wait_for(rest, NQ - 1, rest_sem.at[1])
            gathered0[...] = gathered[...].astype(F32) + rest[...].astype(F32)
            wait_for(update_top, NQ - 1, update_sem.at[1, 1])
            wait_for(update_recv, NQ - 1, update_sem.at[0, 1])
            u = from_steps(update_recv[...], update_top[...])
            squares = jnp.sum(u * u, axis=(0, 1), keepdims=False)[None, :]
            inverse = STEP_SIZE * lax.rsqrt(squares * (1.0 / R) + EPSILON)
            place_rows(gathered0[...] + u * inverse[None])
            block_init[...] += own_update[...] * inverse
        else:
            square_recv[q] = jnp.sum(update * update, axis=0, keepdims=True)
            send_plane(lambda _: square_recv.at[q], square_recv, square_sem)
            wait_for(square_recv, NQ - 1, square_sem.at[1])
            squares = jnp.sum(square_recv[...], axis=0)
            inverse = STEP_SIZE * lax.rsqrt(squares * (1.0 / R) + EPSILON)
            final = block_init[...] + update * inverse
            mine = jnp.zeros((8, C), F32)
            for j in range(4):
                mine = jnp.where(z // 2 == j, final[8 * j : 8 * j + 8], mine)
            mine = jnp.where(z % 2 == 0, mine, swap4(mine))
            final_ref[...] = mine[0:4]

    wait_for(tiles, NZ - 1, tile_sem.at[0])
    wait_for(gathered, NQ - 1, block_sem.at[0])
    wait_for(rest, NQ - 1, rest_sem.at[0])
    wait_for(update_recv, NQ - 1, update_sem.at[0, 0])
    wait_for(update_top, NQ - 1, update_sem.at[1, 0])
    wait_for(square_recv, NQ - 1, square_sem.at[0])
    for sweep in range(2):
        wait_for(part_recv.at[sweep], NQ - 1, part_sem.at[sweep, 0, 0])
        wait_for(part_top.at[sweep], NQ - 1, part_sem.at[sweep, 1, 0])
        wait_for(zsum_recv.at[sweep], NZ - 1, zsum_sem.at[sweep, 0, 0])
        wait_for(zsum_top.at[sweep], NZ - 1, zsum_sem.at[sweep, 1, 0])
    store.wait()


def on_device(coef_init, basis, basis_scale, ext_force, precond, connectivity, halo_nodes, plastic):
    vmem = pl.BlockSpec(memory_space=pltpu.VMEM)
    smem = pl.BlockSpec(memory_space=pltpu.SMEM)
    anywhere = pl.BlockSpec(memory_space=pl.ANY)
    dma = pltpu.SemaphoreType.DMA
    return pl.pallas_call(
        kernel,
        out_shape=(jax.ShapeDtypeStruct((4, C), F32), jax.ShapeDtypeStruct((ROWS, C), F32)),
        in_specs=[vmem, smem, smem, vmem, vmem, vmem, anywhere, anywhere],
        out_specs=(vmem, anywhere),
        scratch_shapes=[
            pltpu.VMEM((ROWS, R), BF16),
            pltpu.VMEM((ROWS, C), F32),
            pltpu.VMEM((ROWS, ROWS), BF16),
            pltpu.VMEM((ROWS, R), BF16),
            pltpu.VMEM((R, ROWS), BF16),
            pltpu.VMEM((ROWS, C), F32),
            pltpu.VMEM((6, LAYER, C), F32),
            pltpu.VMEM((6, LAYER + 16, C), F32),
            pltpu.VMEM((ROWS, C), F32),
            pltpu.VMEM((12, LAYER + 16, C), F32),
            pltpu.VMEM((3, LAYER, C), F32),
            pltpu.VMEM((16, 512), F32),
            pltpu.VMEM((NZ, 8, C), F32),
            pltpu.VMEM((BLOCK, C), F32),
            pltpu.VMEM((BLOCK, C), F32),
            pltpu.VMEM((NQ, BLOCK, C), BF16),
            pltpu.VMEM((NQ, BLOCK, C), F32),
            pltpu.VMEM((R, C), BF16),
            pltpu.VMEM((ROWS, C), BF16),
            pltpu.VMEM((2, 2, 3, LAYER, C), jnp.int16),
            pltpu.VMEM((2, 2, 3, LAYER, C), jnp.int16),
            pltpu.VMEM((LAYER, C), BF16),
            pltpu.VMEM((LAYER, C), BF16),
            pltpu.VMEM((16, 2, BLOCK, C), F32),
            pltpu.VMEM((2, NQ, BLOCK, C), jnp.int16),
            pltpu.VMEM((2, NQ, BLOCK, C), jnp.int16),
            pltpu.VMEM((2, NZ, BLOCK, C), jnp.int16),
            pltpu.VMEM((NQ, BLOCK, C), jnp.int16),
            pltpu.VMEM((NQ, 1, C), F32),
            pltpu.VMEM((BLOCK, C), F32),
            pltpu.VMEM((NQ, BLOCK, C), BF16),
            pltpu.VMEM((2, 4, 1, C), F32),
            pltpu.VMEM((2, NQ, 1, C), F32),
            pltpu.VMEM((2, NZ, 1, C), F32),
            pltpu.VMEM((NQ, 1, C), F32),
            dma((3,)),
            dma((2,)),
            dma((2,)),
            dma((2, 2, 2, 2)),
            dma((2,)),
            dma((2, 2, 2)),
            dma((2, 2, 2)),
            dma((2, 2)),
            dma((2,)),
            dma((2,)),
        ],
        compiler_params=pltpu.CompilerParams(
            collective_id=0, has_side_effects=True, vmem_limit_bytes=56 << 20
        ),
        cost_estimate=pl.CostEstimate(flops=14_000_000_000, bytes_accessed=6_000_000, transcendentals=0),
        name="galerkin",
    )(
        coef_init, basis_scale, precond, connectivity.T, halo_nodes.reshape(1, LAYER), plastic.reshape(1, ELEMS),
        basis, ext_force,
    )


def solution(mesh):
    return jax.shard_map(
        on_device,
        mesh=mesh,
        in_specs=(
            P("dom", None), P("dom", None), P("dom"), P("dom", None), P("dom"), P("dom", None), P("dom"), P("dom"),
        ),
        out_specs=(P("dom", None), P("dom", None)),
        check_vma=False,
    )
```

```python
import functools

import jax
import jax.numpy as jnp
from jax import lax
from jax.experimental import pallas as pl
from jax.experimental.pallas import tpu as pltpu
from jax.sharding import PartitionSpec as P

MESH = pl.DeviceIdType.MESH
F32, BF16 = jnp.float32, jnp.bfloat16

R = 1024
C = 128
ROWS = 1536
LAYER = 256
ELEMS = 450
NDEV = 256
NZ = 8
NQ = 32
BLOCK = 32
CHUNK = 32
STEP_SIZE = 0.5
EPSILON = 1e-05


def dot(a, b):
    return jnp.dot(a, b, preferred_element_type=F32)


def split3(x):
    hi = x.astype(BF16)
    rest = x - hi.astype(F32)
    mid = rest.astype(BF16)
    low = (rest - mid.astype(F32)).astype(BF16)
    return jnp.concatenate([hi, mid, low], axis=1)


def peak(x):
    x = jnp.abs(x)
    for _ in range(x.ndim - 2):
        x = jnp.max(x, axis=0)
    return jnp.maximum(jnp.max(x, axis=0, keepdims=True), 1e-30)


def to_steps(x, top):
    return jnp.round(x * (32767.0 / top)).astype(jnp.int32).astype(jnp.int16)


def from_steps(steps, top):
    return steps.astype(jnp.int32).astype(F32) * (top * (1.0 / 32767.0))


def iota(shape, axis):
    return lax.broadcasted_iota(jnp.int32, shape, axis)


def swap4(x):
    return pltpu.roll(x, 4, x.ndim - 2)


def low_half(shape):
    return iota(shape, len(shape) - 2) % 8 < 4


def kernel(
    coef_ref, scale_ref, precond_ref, conn_ref, halo_ref, plastic_ref, basis_hbm, ext_hbm,
    final_ref, out_local,
    basis, ext, sel, grid_basis, grid_basis_t, scale, grid_ext, resid, disp, weight, conn, nodes,
    tiles, block_init, precond32, gathered, gathered0, coef_low, scaled,
    halo_send, halo_recv, weight_send, weight_recv,
    reduced, part_send, part_recv, zsum_recv, update_recv, square_recv, own_update,
    rest, halo_top, part_top, zsum_top, update_top,
    local_sem, tile_sem, block_sem, halo_sem, weight_sem, part_sem, zsum_sem, update_sem, square_sem, rest_sem,
):
    me = lax.axis_index("dom")
    z, q = me // NQ, me % NQ
    nxt, prv = (me + 1) % NDEV, (me + NDEV - 1) % NDEV

    load_basis = pltpu.make_async_copy(basis_hbm, basis, local_sem.at[0])
    load_ext = pltpu.make_async_copy(ext_hbm, ext, local_sem.at[1])
    load_basis.start()
    load_ext.start()

    def in_plane(j):
        return z * NQ + (q + j) % NQ

    def in_column(j):
        return ((z + j) % NZ) * NQ + q

    barrier = pltpu.get_barrier_semaphore()

    def greet_plane(j, c):
        pl.semaphore_signal(barrier, inc=1, device_id=(in_plane(j),), device_id_type=MESH)
        return c

    def greet_column(j, c):
        pl.semaphore_signal(barrier, inc=1, device_id=(in_column(j),), device_id_type=MESH)
        return c

    lax.fori_loop(1, NQ, greet_plane, 0)
    lax.fori_loop(1, NZ, greet_column, 0)
    pl.semaphore_signal(barrier, inc=1, device_id=(nxt,), device_id_type=MESH)
    pl.semaphore_signal(barrier, inc=1, device_id=(prv,), device_id_type=MESH)

    tiles[z, 0:4, :] = coef_ref[...]
    row4 = iota((4, C), 0)
    pre = jnp.zeros((4, C), F32)
    for k in range(4):
        pre = jnp.where(row4 == k, precond_ref[k], pre)
    tiles[z, 4:8, :] = pre

    pl.semaphore_wait(barrier, NQ - 1 + NZ - 1 + 2)

    pending = []

    def send_column(src, buf, sems):
        pending.append((buf, NZ - 1, sems.at[0]))

        def body(j, c):
            pltpu.make_async_remote_copy(
                src, buf.at[z], sems.at[0], sems.at[1], device_id=(in_column(j),), device_id_type=MESH
            ).start()
            return c

        lax.fori_loop(1, NZ, body, 0)

    def send_plane(src_of, buf, sems):
        pending.append((buf, NQ - 1, sems.at[0]))

        def body(j, c):
            pltpu.make_async_remote_copy(
                src_of((q + j) % NQ), buf.at[q], sems.at[0], sems.at[1], device_id=(in_plane(j),), device_id_type=MESH
            ).start()
            return c

        lax.fori_loop(1, NQ, body, 0)

    def wait_for(buf, count, sem):
        part = buf.at[pl.ds(0, count)]
        pltpu.make_async_copy(part, part, sem).wait()

    send_column(tiles.at[z], tiles, tile_sem)

    conn[...] = jnp.full(conn.shape, -1.0, F32)
    conn[0:8, 0:ELEMS] = conn_ref[...].astype(F32)
    conn[8:9, 0:ELEMS] = plastic_ref[...].astype(F32)
    halo_row = halo_ref[...].astype(F32)

    def decode(c, carry):
        at = pl.multiple_of(c * 32, 32)
        rows = pl.ds(at, 32)
        place = (iota((32, 512), 0) + (at + 512)).astype(F32)
        found = jnp.full((32, 512), -1.0, F32)
        for a in range(4):
            found = jnp.maximum(found, jnp.where(conn[4 + a : 5 + a, :] == place, conn[a : a + 1, :], -1.0))
        node1 = jnp.max(found, axis=1, keepdims=True)
        mine = iota((32, LAYER), 0) + at == iota((32, LAYER), 1)
        node0 = jnp.sum(jnp.where(mine, halo_row, 0.0), axis=1, keepdims=True)
        flags = conn[8:9, :]
        flag1 = jnp.sum(jnp.where(conn[0:1, :] == node0, flags, 0.0), axis=1, keepdims=True)
        flag2 = jnp.sum(jnp.where(conn[4:5, :] == place, flags, 0.0), axis=1, keepdims=True)
        cell = iota((32, C), 0) + at
        valid = (cell % 16 < 15) & (cell // 16 < 15)
        weight[1, rows, :] = jnp.where(valid, 1.0 + flag1, 0.0)
        second = jnp.where(valid, 1.0 + flag2, 0.0)
        weight[2, rows, :] = second
        weight_send[rows, :] = second.astype(BF16)
        nodes[rows, :] = jnp.broadcast_to(node0 * 3.0, (32, C)).astype(jnp.int32)
        nodes[pl.ds(pl.multiple_of(LAYER + c * 32, 32), 32), :] = jnp.broadcast_to(node1 * 3.0, (32, C)).astype(jnp.int32)
        return carry

    lax.fori_loop(0, LAYER // 32, decode, 0)

    to_next = pltpu.make_async_remote_copy(
        weight_send, weight_recv, weight_sem.at[0], weight_sem.at[1], device_id=(nxt,), device_id_type=MESH
    )
    to_next.start()

    lane = iota((16, C), 1)

    def select(c, carry):
        node3 = nodes[pl.ds(pl.multiple_of(c * 16, 16), 16), :]
        for i in range(3):
            rows = pl.ds(pl.multiple_of((c // 16 * 3 + i) * LAYER + c % 16 * 16, 16), 16)
            away = node3 + i - lane
            for t in range(ROWS // C):
                sel[rows, C * t : C * t + C] = jnp.where(away == C * t, 1.0, 0.0).astype(BF16)
        return carry

    lax.fori_loop(0, 32, select, 0)

    wait_for(tiles, NZ - 1, tile_sem.at[1])
    low = low_half((8, C))
    for j in range(4):
        a, b = tiles[2 * j], tiles[2 * j + 1]
        block_init[8 * j : 8 * j + 8, :] = jnp.where(low, a, swap4(b))
        precond32[8 * j : 8 * j + 8, :] = jnp.where(low, swap4(a), b)
    first = block_init[...].astype(BF16)
    gathered[q] = first
    send_plane(lambda _: gathered.at[q], gathered, block_sem)
    rest[q] = (block_init[...] - first.astype(F32)).astype(BF16)
    send_plane(lambda _: rest.at[q], rest, rest_sem)

    load_basis.wait()

    def permute(c, carry):
        rows = pl.ds(pl.multiple_of(c * 768, 768), 768)
        grid_basis[rows, :] = dot(sel[rows, :], basis[...]).astype(BF16)
        return carry

    lax.fori_loop(0, 2, permute, 0)

    def scales(c, carry):
        node3 = nodes[pl.ds(pl.multiple_of(c * 16, 16), 16), :]
        for i in range(3):
            tile = (node3 + i) >> 7
            value = jnp.zeros((16, C), F32)
            for t in range(12):
                value = jnp.where(tile == t, scale_ref[t], value)
            scale[pl.ds(pl.multiple_of((c // 16 * 3 + i) * LAYER + c % 16 * 16, 16), 16), :] = value
        return carry

    lax.fori_loop(0, 32, scales, 0)

    zero_rows = jnp.zeros((16, C), F32)
    for k in range(12):
        disp[k, LAYER : LAYER + 16, :] = zero_rows
    for k in range(6):
        resid[k, LAYER : LAYER + 16, :] = zero_rows

    def place_rows(values):
        v = values.reshape(16, 2, 4, 8, C)
        first, second = v[:, 0], v[:, 1]
        mask = low_half((16, 4, 8, C))
        even = jnp.where(mask, first, swap4(second))
        odd = jnp.where(mask, swap4(first), second)
        for j in range(4):
            coef_low[256 * j : 256 * j + 128, :] = even[:, j].reshape(128, C).astype(BF16)
            coef_low[256 * j + 128 : 256 * j + 256, :] = odd[:, j].reshape(128, C).astype(BF16)

    wait_for(gathered, NQ - 1, block_sem.at[1])
    place_rows(gathered[...].astype(F32))

    def elements(k):
        def body(c, carry):
            at = pl.multiple_of(c * CHUNK, CHUNK)
            node_rows = pl.ds(at, CHUNK + 16)
            n = CHUNK + 16
            grad = []
            for i in range(3):
                under, over = disp[3 * k + i, node_rows, :], disp[3 * k + 3 + i, node_rows, :]
                under1, over1 = pltpu.roll(under, n - 1, 0), pltpu.roll(over, n - 1, 0)
                both, both1 = under + over, under1 + over1
                dx = both1 - both
                sx = both1 + both
                sz = (over1 + over) - (under1 + under)
                grad.append((dx[16:] + dx[:CHUNK], sx[16:] - sx[:CHUNK], sz[16:] + sz[:CHUNK]))
            w = weight[k, pl.ds(at, CHUNK), :]
            third = (grad[0][0] + grad[1][1] + grad[2][2]) * (1.0 / 6.0)
            sxx = grad[0][0] * 0.5 - third
            syy = grad[1][1] * 0.5 - third
            szz = grad[2][2] * 0.5 - third
            sxy = (grad[0][1] + grad[1][0]) * 0.25
            sxz = (grad[0][2] + grad[2][0]) * 0.25
            syz = (grad[1][2] + grad[2][1]) * 0.25
            mag2 = sxx * sxx + syy * syy + szz * szz + 2.0 * (sxy * sxy + sxz * sxz + syz * syz)
            plastic = 0.05 + 0.6 * lax.rsqrt(jnp.maximum(mag2, 9.0))
            factor = jnp.where(w > 1.5, plastic, jnp.where(w > 0.5, 0.25, 0.0))
            vol = jnp.where(w > 0.5, third * 0.5625, 0.0)
            stress = {
                (0, 0): vol + factor * sxx, (1, 1): vol + factor * syy, (2, 2): vol + factor * szz,
                (0, 1): factor * sxy, (0, 2): factor * sxz, (1, 2): factor * syz,
            }
            back = {ij: pltpu.roll(s, 1, 0) for ij, s in stress.items()}
            pad = jnp.zeros((16, C), F32)
            for i in range(3):
                ix, iy, iz = (0, i), (min(i, 1), max(i, 1)), (i, 2)
                dx = back[ix] - stress[ix]
                sy = back[iy] + stress[iy]
                sz = back[iz] + stress[iz]
                near, far = dx - sy, dx + sy
                if k >= 1:
                    rows = (3 * (k - 1) + i, node_rows, slice(None))
                    resid[rows] -= jnp.concatenate([near - sz, pad], 0) + jnp.concatenate([pad, far - sz], 0)
                if k <= 1:
                    rows = (3 * k + i, node_rows, slice(None))
                    resid[rows] -= jnp.concatenate([near + sz, pad], 0) + jnp.concatenate([pad, far + sz], 0)
            return carry

        lax.fori_loop(0, LAYER // CHUNK, body, 0)

    for sweep in range(2):
        copies = []
        for layer, (there, side) in enumerate(((prv, 1), (nxt, 0))):
            top = jnp.full((1, C), 1e-30, F32)
            for i in range(3):
                rows = slice((3 * layer + i) * LAYER, (3 * layer + i + 1) * LAYER)
                u = dot(grid_basis[rows, :], coef_low[...]) * scale[rows, :]
                disp[3 + 3 * layer + i, 0:LAYER, :] = u
                top = jnp.maximum(top, peak(u))
            u = disp[3 + 3 * layer : 6 + 3 * layer, 0:LAYER, :]
            halo_top[sweep, layer] = top
            halo_send[sweep, layer] = to_steps(u, top)
            for src, dst, sem in (
                (halo_send.at[sweep, layer], halo_recv.at[sweep, side], 0),
                (halo_top.at[sweep, layer], halo_top.at[sweep, 2 + side], 1),
            ):
                copy = pltpu.make_async_remote_copy(
                    src, dst, halo_sem.at[sweep, layer, sem, 0], halo_sem.at[sweep, layer, sem, 1],
                    device_id=(there,), device_id_type=MESH,
                )
                copy.start()
                copies.append(copy)

        if sweep == 0:
            load_ext.wait()
            ext3 = split3(ext[...])

            def permute_ext(c, carry):
                rows = pl.ds(pl.multiple_of(c * LAYER, LAYER), LAYER)
                e = dot(sel[rows, :], ext3)
                grid_ext[c] = e[:, 0:C] + e[:, C : 2 * C] + e[:, 2 * C :]
                return carry

            lax.fori_loop(0, 6, permute_ext, 0)

            def turn(c, carry):
                rows = pl.ds(pl.multiple_of(c * LAYER, LAYER), LAYER)
                for b in range(4):
                    grid_basis_t[b * 256 : b * 256 + 256, rows] = grid_basis[rows, b * 256 : b * 256 + 256].T
                return carry

            lax.fori_loop(0, 6, turn, 0)
            to_next.wait()
            weight[0] = jnp.where(me > 0, weight_recv[...].astype(F32), 0.0)

        resid[:, 0:LAYER, :] = grid_ext[...]
        elements(1)
        for copy in copies:
            copy.wait()
        disp[0:3, 0:LAYER, :] = from_steps(halo_recv[sweep, 0], halo_top[sweep, 2][None])
        disp[9:12, 0:LAYER, :] = jnp.where(
            me < NDEV - 1, from_steps(halo_recv[sweep, 1], halo_top[sweep, 3][None]), 0.0
        )
        elements(0)
        elements(2)
        for k in range(6):
            rows = slice(k * LAYER, (k + 1) * LAYER)
            scaled[rows, :] = (resid[k, 0:LAYER, :] * scale[rows, :]).astype(BF16)

        mask = low_half((16, 8, C))
        for j in range(4):
            r = dot(grid_basis_t[256 * j : 256 * j + 256, :], scaled[...]).reshape(2, 16, 8, C)
            even, odd = r[0], r[1]
            reduced[:, 0, 8 * j : 8 * j + 8, :] = jnp.where(mask, even, swap4(odd))
            reduced[:, 1, 8 * j : 8 * j + 8, :] = jnp.where(mask, swap4(even), odd)
        parts = reduced[...].reshape(NQ, BLOCK, C)
        top = peak(parts)
        part_top[sweep, q] = top
        part_send[sweep] = to_steps(parts, top[None])
        part_recv[sweep, q] = part_send[sweep, q]
        send_plane(lambda t: part_send.at[sweep, t], part_recv.at[sweep], part_sem.at[sweep, 0])
        send_plane(lambda _: part_top.at[sweep, q], part_top.at[sweep], part_sem.at[sweep, 1])

        if sweep == 1:
            out_local[...] = jnp.zeros_like(out_local)

            def restore(c, carry):
                rows = pl.ds(pl.multiple_of(c * LAYER, LAYER), LAYER)
                o = lax.dot_general(
                    sel[rows, :], split3(resid[c, 0:LAYER, :]), (((0,), (0,)), ((), ())), preferred_element_type=F32
                )
                out_local[...] += o[:, 0:C] + o[:, C : 2 * C] + o[:, 2 * C :]
                return carry

            lax.fori_loop(0, 6, restore, 0)

        wait_for(part_recv.at[sweep], NQ - 1, part_sem.at[sweep, 0, 1])
        wait_for(part_top.at[sweep], NQ - 1, part_sem.at[sweep, 1, 1])
        total = from_steps(part_recv[sweep, 0], part_top[sweep, 0])
        for t in range(1, NQ):
            total += from_steps(part_recv[sweep, t], part_top[sweep, t])
        top = peak(total)
        zsum_top[sweep, z] = top
        zsum_recv[sweep, z] = to_steps(total, top)
        send_column(zsum_recv.at[sweep, z], zsum_recv.at[sweep], zsum_sem.at[sweep, 0])
        send_column(zsum_top.at[sweep, z], zsum_top.at[sweep], zsum_sem.at[sweep, 1])
        wait_for(zsum_top.at[sweep], NZ - 1, zsum_sem.at[sweep, 1, 1])
        wait_for(zsum_recv.at[sweep], NZ - 1, zsum_sem.at[sweep, 0, 1])
        total = from_steps(zsum_recv[sweep, 0], zsum_top[sweep, 0])
        for t in range(1, NZ):
            total += from_steps(zsum_recv[sweep, t], zsum_top[sweep, t])
        update = total * precond32[...]

        if sweep == 0:
            own_update[...] = update
            top = peak(update)
            update_top[q] = top
            update_recv[q] = to_steps(update, top)
            send_plane(lambda _: update_recv.at[q], update_recv, update_sem.at[0])
            send_plane(lambda _: update_top.at[q], update_top, update_sem.at[1])
            wait_for(rest, NQ - 1, rest_sem.at[1])
            gathered0[...] = gathered[...].astype(F32) + rest[...].astype(F32)
            wait_for(update_top, NQ - 1, update_sem.at[1, 1])
            wait_for(update_recv, NQ - 1, update_sem.at[0, 1])
            u = from_steps(update_recv[...], update_top[...])
            squares = jnp.sum(u * u, axis=(0, 1), keepdims=False)[None, :]
            inverse = STEP_SIZE * lax.rsqrt(squares * (1.0 / R) + EPSILON)
            place_rows(gathered0[...] + u * inverse[None])
            block_init[...] += own_update[...] * inverse
        else:
            square_recv[q] = jnp.sum(update * update, axis=0, keepdims=True)
            send_plane(lambda _: square_recv.at[q], square_recv, square_sem)
            wait_for(square_recv, NQ - 1, square_sem.at[1])
            squares = jnp.sum(square_recv[...], axis=0)
            inverse = STEP_SIZE * lax.rsqrt(squares * (1.0 / R) + EPSILON)
            final = block_init[...] + update * inverse
            mine = jnp.zeros((8, C), F32)
            for j in range(4):
                mine = jnp.where(z // 2 == j, final[8 * j : 8 * j + 8], mine)
            mine = jnp.where(z % 2 == 0, mine, swap4(mine))
            final_ref[...] = mine[0:4]

    for sent in pending:
        wait_for(*sent)


def on_device(coef_init, basis, basis_scale, ext_force, precond, connectivity, halo_nodes, plastic):
    vmem = pl.BlockSpec(memory_space=pltpu.VMEM)
    smem = pl.BlockSpec(memory_space=pltpu.SMEM)
    anywhere = pl.BlockSpec(memory_space=pl.ANY)
    dma = pltpu.SemaphoreType.DMA
    return pl.pallas_call(
        kernel,
        out_shape=(pltpu.VMEM((4, C), F32), pltpu.VMEM((ROWS, C), F32)),
        in_specs=[vmem, smem, smem, vmem, vmem, vmem, anywhere, anywhere],
        out_specs=(vmem, vmem),
        scratch_shapes=[
            pltpu.VMEM((ROWS, R), BF16),
            pltpu.VMEM((ROWS, C), F32),
            pltpu.VMEM((ROWS, ROWS), BF16),
            pltpu.VMEM((ROWS, R), BF16),
            pltpu.VMEM((R, ROWS), BF16),
            pltpu.VMEM((ROWS, C), F32),
            pltpu.VMEM((6, LAYER, C), F32),
            pltpu.VMEM((6, LAYER + 16, C), F32),
            pltpu.VMEM((12, LAYER + 16, C), F32),
            pltpu.VMEM((3, LAYER, C), F32),
            pltpu.VMEM((16, 512), F32),
            pltpu.VMEM((2 * LAYER, C), jnp.int32),
            pltpu.VMEM((NZ, 8, C), F32),
            pltpu.VMEM((BLOCK, C), F32),
            pltpu.VMEM((BLOCK, C), F32),
            pltpu.VMEM((NQ, BLOCK, C), BF16),
            pltpu.VMEM((NQ, BLOCK, C), F32),
            pltpu.VMEM((R, C), BF16),
            pltpu.VMEM((ROWS, C), BF16),
            pltpu.VMEM((2, 2, 3, LAYER, C), jnp.int16),
            pltpu.VMEM((2, 2, 3, LAYER, C), jnp.int16),
            pltpu.VMEM((LAYER, C), BF16),
            pltpu.VMEM((LAYER, C), BF16),
            pltpu.VMEM((16, 2, BLOCK, C), F32),
            pltpu.VMEM((2, NQ, BLOCK, C), jnp.int16),
            pltpu.VMEM((2, NQ, BLOCK, C), jnp.int16),
            pltpu.VMEM((2, NZ, BLOCK, C), jnp.int16),
            pltpu.VMEM((NQ, BLOCK, C), jnp.int16),
            pltpu.VMEM((NQ, 1, C), F32),
            pltpu.VMEM((BLOCK, C), F32),
            pltpu.VMEM((NQ, BLOCK, C), BF16),
            pltpu.VMEM((2, 4, 1, C), F32),
            pltpu.VMEM((2, NQ, 1, C), F32),
            pltpu.VMEM((2, NZ, 1, C), F32),
            pltpu.VMEM((NQ, 1, C), F32),
            dma((2,)),
            dma((2,)),
            dma((2,)),
            dma((2, 2, 2, 2)),
            dma((2,)),
            dma((2, 2, 2)),
            dma((2, 2, 2)),
            dma((2, 2)),
            dma((2,)),
            dma((2,)),
        ],
        compiler_params=pltpu.CompilerParams(
            collective_id=0, has_side_effects=True, vmem_limit_bytes=58 << 20
        ),
        cost_estimate=pl.CostEstimate(flops=14_000_000_000, bytes_accessed=6_000_000, transcendentals=0),
        name="galerkin",
    )(
        coef_init, basis_scale, precond, connectivity.T, halo_nodes.reshape(1, LAYER), plastic.reshape(1, ELEMS),
        basis, ext_force,
    )


def solution(mesh):
    return jax.shard_map(
        on_device,
        mesh=mesh,
        in_specs=(
            P("dom", None), P("dom", None), P("dom"), P("dom", None), P("dom"), P("dom", None), P("dom"), P("dom"),
        ),
        out_specs=(P("dom", None), P("dom", None)),
        check_vma=False,
    )
```

```python
import functools

import jax
import jax.numpy as jnp
from jax import lax
from jax.experimental import pallas as pl
from jax.experimental.pallas import tpu as pltpu
from jax.sharding import PartitionSpec as P

MESH = pl.DeviceIdType.MESH
F32, BF16 = jnp.float32, jnp.bfloat16

R = 1024
C = 128
ROWS = 1536
LAYER = 256
ELEMS = 450
NDEV = 256
NZ = 8
NQ = 32
BLOCK = 32
CHUNK = 32
STEP_SIZE = 0.5
EPSILON = 1e-05


def dot(a, b):
    return jnp.dot(a, b, preferred_element_type=F32)


def split3(x):
    hi = x.astype(BF16)
    rest = x - hi.astype(F32)
    mid = rest.astype(BF16)
    low = (rest - mid.astype(F32)).astype(BF16)
    return jnp.concatenate([hi, mid, low], axis=1)


def peak(x):
    x = jnp.abs(x)
    for _ in range(x.ndim - 2):
        x = jnp.max(x, axis=0)
    return jnp.maximum(jnp.max(x, axis=0, keepdims=True), 1e-30)


def to_steps(x, top):
    return jnp.round(x * (32767.0 / top)).astype(jnp.int32).astype(jnp.int16)


def from_steps(steps, top):
    return steps.astype(jnp.int32).astype(F32) * (top * (1.0 / 32767.0))


def iota(shape, axis):
    return lax.broadcasted_iota(jnp.int32, shape, axis)


def swap4(x):
    return pltpu.roll(x, 4, x.ndim - 2)


def low_half(shape):
    return iota(shape, len(shape) - 2) % 8 < 4


def kernel(
    coef_ref, scale_ref, precond_ref, conn_ref, halo_ref, plastic_ref, basis_hbm, ext_hbm,
    final_ref, out_local,
    basis, ext, sel, grid_basis, grid_basis_t, scale, grid_ext, resid, disp, weight, conn, nodes,
    tiles, block_init, precond32, gathered, gathered0, coef_low, scaled,
    halo_send, halo_recv, weight_send, weight_recv,
    reduced, part_send, part_recv, zsum_recv, update_recv, square_recv, own_update,
    rest, halo_top, part_top, zsum_top, update_top,
    local_sem, tile_sem, block_sem, halo_sem, weight_sem, part_sem, zsum_sem, update_sem, square_sem, rest_sem,
):
    me = lax.axis_index("dom")
    z, q = me // NQ, me % NQ
    nxt, prv = (me + 1) % NDEV, (me + NDEV - 1) % NDEV

    load_basis = pltpu.make_async_copy(basis_hbm, basis, local_sem.at[0])
    load_ext = pltpu.make_async_copy(ext_hbm, ext, local_sem.at[1])
    load_basis.start()
    load_ext.start()

    def in_plane(j):
        return z * NQ + (q + j) % NQ

    def in_column(j):
        return ((z + j) % NZ) * NQ + q

    barrier = pltpu.get_barrier_semaphore()

    def greet_plane(j, c):
        pl.semaphore_signal(barrier, inc=1, device_id=(in_plane(j),), device_id_type=MESH)
        return c

    def greet_column(j, c):
        pl.semaphore_signal(barrier, inc=1, device_id=(in_column(j),), device_id_type=MESH)
        return c

    lax.fori_loop(1, NQ, greet_plane, 0)
    lax.fori_loop(1, NZ, greet_column, 0)
    pl.semaphore_signal(barrier, inc=1, device_id=(nxt,), device_id_type=MESH)
    pl.semaphore_signal(barrier, inc=1, device_id=(prv,), device_id_type=MESH)

    tiles[z, 0:4, :] = coef_ref[...]
    row4 = iota((4, C), 0)
    pre = jnp.zeros((4, C), F32)
    for k in range(4):
        pre = jnp.where(row4 == k, precond_ref[k], pre)
    tiles[z, 4:8, :] = pre

    pl.semaphore_wait(barrier, NQ - 1 + NZ - 1 + 2)

    pending = []

    def send_column(src, buf, sems):
        pending.append((buf, NZ - 1, sems.at[0]))

        def body(j, c):
            pltpu.make_async_remote_copy(
                src, buf.at[z], sems.at[0], sems.at[1], device_id=(in_column(j),), device_id_type=MESH
            ).start()
            return c

        lax.fori_loop(1, NZ, body, 0)

    def send_plane(src_of, buf, sems):
        pending.append((buf, NQ - 1, sems.at[0]))

        def body(j, c):
            pltpu.make_async_remote_copy(
                src_of((q + j) % NQ), buf.at[q], sems.at[0], sems.at[1], device_id=(in_plane(j),), device_id_type=MESH
            ).start()
            return c

        lax.fori_loop(1, NQ, body, 0)

    def wait_for(buf, count, sem):
        part = buf.at[pl.ds(0, count)]
        pltpu.make_async_copy(part, part, sem).wait()

    send_column(tiles.at[z], tiles, tile_sem)

    conn[...] = jnp.full(conn.shape, -1.0, F32)
    conn[0:8, 0:ELEMS] = conn_ref[...].astype(F32)
    conn[8:9, 0:ELEMS] = plastic_ref[...].astype(F32)
    halo_row = halo_ref[...].astype(F32)

    def decode(c, carry):
        at = pl.multiple_of(c * 32, 32)
        rows = pl.ds(at, 32)
        place = (iota((32, 512), 0) + (at + 512)).astype(F32)
        found = jnp.full((32, 512), -1.0, F32)
        for a in range(4):
            found = jnp.maximum(found, jnp.where(conn[4 + a : 5 + a, :] == place, conn[a : a + 1, :], -1.0))
        node1 = jnp.max(found, axis=1, keepdims=True)
        mine = iota((32, LAYER), 0) + at == iota((32, LAYER), 1)
        node0 = jnp.sum(jnp.where(mine, halo_row, 0.0), axis=1, keepdims=True)
        flags = conn[8:9, :]
        flag1 = jnp.sum(jnp.where(conn[0:1, :] == node0, flags, 0.0), axis=1, keepdims=True)
        flag2 = jnp.sum(jnp.where(conn[4:5, :] == place, flags, 0.0), axis=1, keepdims=True)
        cell = iota((32, C), 0) + at
        valid = (cell % 16 < 15) & (cell // 16 < 15)
        weight[1, rows, :] = jnp.where(valid, 1.0 + flag1, 0.0)
        second = jnp.where(valid, 1.0 + flag2, 0.0)
        weight[2, rows, :] = second
        weight_send[rows, :] = second.astype(BF16)
        nodes[rows, :] = jnp.broadcast_to(node0 * 3.0, (32, C)).astype(jnp.int32)
        nodes[pl.ds(pl.multiple_of(LAYER + c * 32, 32), 32), :] = jnp.broadcast_to(node1 * 3.0, (32, C)).astype(jnp.int32)
        return carry

    lax.fori_loop(0, LAYER // 32, decode, 0)

    to_next = pltpu.make_async_remote_copy(
        weight_send, weight_recv, weight_sem.at[0], weight_sem.at[1], device_id=(nxt,), device_id_type=MESH
    )
    to_next.start()

    lane = iota((16, C), 1)

    def select(c, carry):
        node3 = nodes[pl.ds(pl.multiple_of(c * 16, 16), 16), :]
        for i in range(3):
            rows = pl.ds(pl.multiple_of((c // 16 * 3 + i) * LAYER + c % 16 * 16, 16), 16)
            away = node3 + i - lane
            for t in range(ROWS // C):
                sel[rows, C * t : C * t + C] = jnp.where(away == C * t, 1.0, 0.0).astype(BF16)
        return carry

    lax.fori_loop(0, 32, select, 0)

    wait_for(tiles, NZ - 1, tile_sem.at[1])
    low = low_half((8, C))
    for j in range(4):
        a, b = tiles[2 * j], tiles[2 * j + 1]
        block_init[8 * j : 8 * j + 8, :] = jnp.where(low, a, swap4(b))
        precond32[8 * j : 8 * j + 8, :] = jnp.where(low, swap4(a), b)
    first = block_init[...].astype(BF16)
    gathered[q] = first
    send_plane(lambda _: gathered.at[q], gathered, block_sem)
    rest[q] = (block_init[...] - first.astype(F32)).astype(BF16)
    send_plane(lambda _: rest.at[q], rest, rest_sem)

    load_basis.wait()

    def permute(c, carry):
        rows = pl.ds(pl.multiple_of(c * 768, 768), 768)
        grid_basis[rows, :] = dot(sel[rows, :], basis[...]).astype(BF16)
        return carry

    lax.fori_loop(0, 2, permute, 0)

    def scales(c, carry):
        node3 = nodes[pl.ds(pl.multiple_of(c * 16, 16), 16), :]
        for i in range(3):
            tile = (node3 + i) >> 7
            value = jnp.zeros((16, C), F32)
            for t in range(12):
                value = jnp.where(tile == t, scale_ref[t], value)
            scale[pl.ds(pl.multiple_of((c // 16 * 3 + i) * LAYER + c % 16 * 16, 16), 16), :] = value
        return carry

    lax.fori_loop(0, 32, scales, 0)

    zero_rows = jnp.zeros((16, C), F32)
    for k in range(12):
        disp[k, LAYER : LAYER + 16, :] = zero_rows
    for k in range(6):
        resid[k, LAYER : LAYER + 16, :] = zero_rows

    def place_rows(values):
        v = values.reshape(16, 2, 4, 8, C)
        first, second = v[:, 0], v[:, 1]
        mask = low_half((16, 4, 8, C))
        even = jnp.where(mask, first, swap4(second))
        odd = jnp.where(mask, swap4(first), second)
        for j in range(4):
            coef_low[256 * j : 256 * j + 128, :] = even[:, j].reshape(128, C).astype(BF16)
            coef_low[256 * j + 128 : 256 * j + 256, :] = odd[:, j].reshape(128, C).astype(BF16)

    wait_for(gathered, NQ - 1, block_sem.at[1])
    place_rows(gathered[...].astype(F32))

    def elements(k):
        def body(c, carry):
            at = pl.multiple_of(c * CHUNK, CHUNK)
            node_rows = pl.ds(at, CHUNK + 16)
            n = CHUNK + 16
            grad = []
            for i in range(3):
                under, over = disp[3 * k + i, node_rows, :], disp[3 * k + 3 + i, node_rows, :]
                under1, over1 = pltpu.roll(under, n - 1, 0), pltpu.roll(over, n - 1, 0)
                both, both1 = under + over, under1 + over1
                dx = both1 - both
                sx = both1 + both
                sz = (over1 + over) - (under1 + under)
                grad.append((dx[16:] + dx[:CHUNK], sx[16:] - sx[:CHUNK], sz[16:] + sz[:CHUNK]))
            w = weight[k, pl.ds(at, CHUNK), :]
            third = (grad[0][0] + grad[1][1] + grad[2][2]) * (1.0 / 6.0)
            sxx = grad[0][0] * 0.5 - third
            syy = grad[1][1] * 0.5 - third
            szz = grad[2][2] * 0.5 - third
            sxy = (grad[0][1] + grad[1][0]) * 0.25
            sxz = (grad[0][2] + grad[2][0]) * 0.25
            syz = (grad[1][2] + grad[2][1]) * 0.25
            mag2 = sxx * sxx + syy * syy + szz * szz + 2.0 * (sxy * sxy + sxz * sxz + syz * syz)
            plastic = 0.05 + 0.6 * lax.rsqrt(jnp.maximum(mag2, 9.0))
            factor = jnp.where(w > 1.5, plastic, jnp.where(w > 0.5, 0.25, 0.0))
            vol = jnp.where(w > 0.5, third * 0.5625, 0.0)
            stress = {
                (0, 0): vol + factor * sxx, (1, 1): vol + factor * syy, (2, 2): vol + factor * szz,
                (0, 1): factor * sxy, (0, 2): factor * sxz, (1, 2): factor * syz,
            }
            back = {ij: pltpu.roll(s, 1, 0) for ij, s in stress.items()}
            pad = jnp.zeros((16, C), F32)
            for i in range(3):
                ix, iy, iz = (0, i), (min(i, 1), max(i, 1)), (i, 2)
                dx = back[ix] - stress[ix]
                sy = back[iy] + stress[iy]
                sz = back[iz] + stress[iz]
                near, far = dx - sy, dx + sy
                if k >= 1:
                    rows = (3 * (k - 1) + i, node_rows, slice(None))
                    resid[rows] -= jnp.concatenate([near - sz, pad], 0) + jnp.concatenate([pad, far - sz], 0)
                if k <= 1:
                    rows = (3 * k + i, node_rows, slice(None))
                    resid[rows] -= jnp.concatenate([near + sz, pad], 0) + jnp.concatenate([pad, far + sz], 0)
            return carry

        lax.fori_loop(0, LAYER // CHUNK, body, 0)

    sent_pieces = []
    for sweep in range(2):
        pieces = ([], [])
        for i in range(3):
            for layer, (there, side) in enumerate(((prv, 1), (nxt, 0))):
                rows = slice((3 * layer + i) * LAYER, (3 * layer + i + 1) * LAYER)
                u = dot(grid_basis[rows, :], coef_low[...]) * scale[rows, :]
                disp[3 + 3 * layer + i, 0:LAYER, :] = u
                top = peak(u)
                halo_top[sweep, layer, i] = top
                halo_send[sweep, layer, i] = to_steps(u, top)
                for src, dst, kind in (
                    (halo_send.at[sweep, layer, i], halo_recv.at[sweep, side, i], 0),
                    (halo_top.at[sweep, layer, i], halo_top.at[sweep, 2 + side, i], 1),
                ):
                    sems = halo_sem.at[sweep, 6 * layer + 2 * i + kind]
                    copy = pltpu.make_async_remote_copy(
                        src, dst, sems.at[0], sems.at[1], device_id=(there,), device_id_type=MESH
                    )
                    copy.start()
                    pieces[layer].append(copy)

        if sweep == 0:
            load_ext.wait()
            ext3 = split3(ext[...])

            def permute_ext(c, carry):
                rows = pl.ds(pl.multiple_of(c * LAYER, LAYER), LAYER)
                e = dot(sel[rows, :], ext3)
                grid_ext[c] = e[:, 0:C] + e[:, C : 2 * C] + e[:, 2 * C :]
                return carry

            lax.fori_loop(0, 6, permute_ext, 0)

            def turn(c, carry):
                rows = pl.ds(pl.multiple_of(c * LAYER, LAYER), LAYER)
                for b in range(4):
                    grid_basis_t[b * 256 : b * 256 + 256, rows] = grid_basis[rows, b * 256 : b * 256 + 256].T
                return carry

            lax.fori_loop(0, 6, turn, 0)
            to_next.wait()
            weight[0] = jnp.where(me > 0, weight_recv[...].astype(F32), 0.0)

        resid[:, 0:LAYER, :] = grid_ext[...]
        elements(1)
        for layer, side in ((0, 1), (1, 0)):
            for copy in pieces[layer]:
                copy.wait_recv()
            for i in range(3):
                u = from_steps(halo_recv[sweep, side, i], halo_top[sweep, 2 + side, i])
                disp[9 * side + i, 0:LAYER, :] = jnp.where(me < NDEV - 1, u, 0.0) if side == 1 else u
            elements(2 * side)
        sent_pieces += pieces[0] + pieces[1]
        for k in range(6):
            rows = slice(k * LAYER, (k + 1) * LAYER)
            scaled[rows, :] = (resid[k, 0:LAYER, :] * scale[rows, :]).astype(BF16)

        mask = low_half((16, 8, C))
        for j in range(4):
            r = dot(grid_basis_t[256 * j : 256 * j + 256, :], scaled[...]).reshape(2, 16, 8, C)
            even, odd = r[0], r[1]
            reduced[:, 0, 8 * j : 8 * j + 8, :] = jnp.where(mask, even, swap4(odd))
            reduced[:, 1, 8 * j : 8 * j + 8, :] = jnp.where(mask, swap4(even), odd)
        parts = reduced[...].reshape(NQ, BLOCK, C)
        top = peak(parts)
        part_top[sweep, q] = top
        part_send[sweep] = to_steps(parts, top[None])
        part_recv[sweep, q] = part_send[sweep, q]
        send_plane(lambda t: part_send.at[sweep, t], part_recv.at[sweep], part_sem.at[sweep, 0])
        send_plane(lambda _: part_top.at[sweep, q], part_top.at[sweep], part_sem.at[sweep, 1])

        if sweep == 1:
            out_local[...] = jnp.zeros_like(out_local)

            def restore(c, carry):
                rows = pl.ds(pl.multiple_of(c * LAYER, LAYER), LAYER)
                o = lax.dot_general(
                    sel[rows, :], split3(resid[c, 0:LAYER, :]), (((0,), (0,)), ((), ())), preferred_element_type=F32
                )
                out_local[...] += o[:, 0:C] + o[:, C : 2 * C] + o[:, 2 * C :]
                return carry

            lax.fori_loop(0, 6, restore, 0)

        wait_for(part_recv.at[sweep], NQ - 1, part_sem.at[sweep, 0, 1])
        wait_for(part_top.at[sweep], NQ - 1, part_sem.at[sweep, 1, 1])
        total = from_steps(part_recv[sweep, 0], part_top[sweep, 0])
        for t in range(1, NQ):
            total += from_steps(part_recv[sweep, t], part_top[sweep, t])
        top = peak(total)
        zsum_top[sweep, z] = top
        zsum_recv[sweep, z] = to_steps(total, top)
        send_column(zsum_recv.at[sweep, z], zsum_recv.at[sweep], zsum_sem.at[sweep, 0])
        send_column(zsum_top.at[sweep, z], zsum_top.at[sweep], zsum_sem.at[sweep, 1])
        wait_for(zsum_top.at[sweep], NZ - 1, zsum_sem.at[sweep, 1, 1])
        wait_for(zsum_recv.at[sweep], NZ - 1, zsum_sem.at[sweep, 0, 1])
        total = from_steps(zsum_recv[sweep, 0], zsum_top[sweep, 0])
        for t in range(1, NZ):
            total += from_steps(zsum_recv[sweep, t], zsum_top[sweep, t])
        update = total * precond32[...]

        if sweep == 0:
            own_update[...] = update
            top = peak(update)
            update_top[q] = top
            update_recv[q] = to_steps(update, top)
            send_plane(lambda _: update_recv.at[q], update_recv, update_sem.at[0])
            send_plane(lambda _: update_top.at[q], update_top, update_sem.at[1])
            wait_for(rest, NQ - 1, rest_sem.at[1])
            gathered0[...] = gathered[...].astype(F32) + rest[...].astype(F32)
            wait_for(update_top, NQ - 1, update_sem.at[1, 1])
            wait_for(update_recv, NQ - 1, update_sem.at[0, 1])
            u = from_steps(update_recv[...], update_top[...])
            squares = jnp.sum(u * u, axis=(0, 1), keepdims=False)[None, :]
            inverse = STEP_SIZE * lax.rsqrt(squares * (1.0 / R) + EPSILON)
            place_rows(gathered0[...] + u * inverse[None])
            block_init[...] += own_update[...] * inverse
        else:
            square_recv[q] = jnp.sum(update * update, axis=0, keepdims=True)
            send_plane(lambda _: square_recv.at[q], square_recv, square_sem)
            wait_for(square_recv, NQ - 1, square_sem.at[1])
            squares = jnp.sum(square_recv[...], axis=0)
            inverse = STEP_SIZE * lax.rsqrt(squares * (1.0 / R) + EPSILON)
            final = block_init[...] + update * inverse
            mine = jnp.zeros((8, C), F32)
            for j in range(4):
                mine = jnp.where(z // 2 == j, final[8 * j : 8 * j + 8], mine)
            mine = jnp.where(z % 2 == 0, mine, swap4(mine))
            final_ref[...] = mine[0:4]

    for copy in sent_pieces:
        copy.wait_send()
    for sent in pending:
        wait_for(*sent)


def on_device(coef_init, basis, basis_scale, ext_force, precond, connectivity, halo_nodes, plastic):
    vmem = pl.BlockSpec(memory_space=pltpu.VMEM)
    smem = pl.BlockSpec(memory_space=pltpu.SMEM)
    anywhere = pl.BlockSpec(memory_space=pl.ANY)
    dma = pltpu.SemaphoreType.DMA
    return pl.pallas_call(
        kernel,
        out_shape=(pltpu.VMEM((4, C), F32), pltpu.VMEM((ROWS, C), F32)),
        in_specs=[vmem, smem, smem, vmem, vmem, vmem, anywhere, anywhere],
        out_specs=(vmem, vmem),
        scratch_shapes=[
            pltpu.VMEM((ROWS, R), BF16),
            pltpu.VMEM((ROWS, C), F32),
            pltpu.VMEM((ROWS, ROWS), BF16),
            pltpu.VMEM((ROWS, R), BF16),
            pltpu.VMEM((R, ROWS), BF16),
            pltpu.VMEM((ROWS, C), F32),
            pltpu.VMEM((6, LAYER, C), F32),
            pltpu.VMEM((6, LAYER + 16, C), F32),
            pltpu.VMEM((12, LAYER + 16, C), F32),
            pltpu.VMEM((3, LAYER, C), F32),
            pltpu.VMEM((16, 512), F32),
            pltpu.VMEM((2 * LAYER, C), jnp.int32),
            pltpu.VMEM((NZ, 8, C), F32),
            pltpu.VMEM((BLOCK, C), F32),
            pltpu.VMEM((BLOCK, C), F32),
            pltpu.VMEM((NQ, BLOCK, C), BF16),
            pltpu.VMEM((NQ, BLOCK, C), F32),
            pltpu.VMEM((R, C), BF16),
            pltpu.VMEM((ROWS, C), BF16),
            pltpu.VMEM((2, 2, 3, LAYER, C), jnp.int16),
            pltpu.VMEM((2, 2, 3, LAYER, C), jnp.int16),
            pltpu.VMEM((LAYER, C), BF16),
            pltpu.VMEM((LAYER, C), BF16),
            pltpu.VMEM((16, 2, BLOCK, C), F32),
            pltpu.VMEM((2, NQ, BLOCK, C), jnp.int16),
            pltpu.VMEM((2, NQ, BLOCK, C), jnp.int16),
            pltpu.VMEM((2, NZ, BLOCK, C), jnp.int16),
            pltpu.VMEM((NQ, BLOCK, C), jnp.int16),
            pltpu.VMEM((NQ, 1, C), F32),
            pltpu.VMEM((BLOCK, C), F32),
            pltpu.VMEM((NQ, BLOCK, C), BF16),
            pltpu.VMEM((2, 4, 3, 1, C), F32),
            pltpu.VMEM((2, NQ, 1, C), F32),
            pltpu.VMEM((2, NZ, 1, C), F32),
            pltpu.VMEM((NQ, 1, C), F32),
            dma((2,)),
            dma((2,)),
            dma((2,)),
            dma((2, 12, 2)),
            dma((2,)),
            dma((2, 2, 2)),
            dma((2, 2, 2)),
            dma((2, 2)),
            dma((2,)),
            dma((2,)),
        ],
        compiler_params=pltpu.CompilerParams(
            collective_id=0, has_side_effects=True, vmem_limit_bytes=58 << 20
        ),
        cost_estimate=pl.CostEstimate(flops=14_000_000_000, bytes_accessed=6_000_000, transcendentals=0),
        name="galerkin",
    )(
        coef_init, basis_scale, precond, connectivity.T, halo_nodes.reshape(1, LAYER), plastic.reshape(1, ELEMS),
        basis, ext_force,
    )


def solution(mesh):
    return jax.shard_map(
        on_device,
        mesh=mesh,
        in_specs=(
            P("dom", None), P("dom", None), P("dom"), P("dom", None), P("dom"), P("dom", None), P("dom"), P("dom"),
        ),
        out_specs=(P("dom", None), P("dom", None)),
        check_vma=False,
    )
```

```python
import functools

import jax
import jax.numpy as jnp
from jax import lax
from jax.experimental import pallas as pl
from jax.experimental.pallas import tpu as pltpu
from jax.sharding import PartitionSpec as P

MESH = pl.DeviceIdType.MESH
F32, BF16 = jnp.float32, jnp.bfloat16

R = 1024
C = 128
ROWS = 1536
LAYER = 256
ELEMS = 450
NDEV = 256
NZ = 8
NQ = 32
BLOCK = 32
CHUNK = 64
STEP_SIZE = 0.5
EPSILON = 1e-05


def dot(a, b):
    return jnp.dot(a, b, preferred_element_type=F32)


def split3(x):
    hi = x.astype(BF16)
    rest = x - hi.astype(F32)
    mid = rest.astype(BF16)
    low = (rest - mid.astype(F32)).astype(BF16)
    return jnp.concatenate([hi, mid, low], axis=1)


def peak(x):
    x = jnp.abs(x)
    for _ in range(x.ndim - 2):
        x = jnp.max(x, axis=0)
    return jnp.maximum(jnp.max(x, axis=0, keepdims=True), 1e-30)


def to_steps(x, top):
    return jnp.round(x * (32767.0 / top)).astype(jnp.int32).astype(jnp.int16)


def from_steps(steps, top):
    return steps.astype(jnp.int32).astype(F32) * (top * (1.0 / 32767.0))


def iota(shape, axis):
    return lax.broadcasted_iota(jnp.int32, shape, axis)


def swap4(x):
    return pltpu.roll(x, 4, x.ndim - 2)


def low_half(shape):
    return iota(shape, len(shape) - 2) % 8 < 4


def kernel(
    coef_ref, scale_ref, precond_ref, conn_ref, halo_ref, plastic_ref, basis_hbm, ext_hbm,
    final_ref, out_local,
    basis, ext, sel, grid_basis, grid_basis_t, scale, grid_ext, resid, disp, weight, conn, nodes,
    tiles, block_init, precond32, gathered, gathered0, coef_low, scaled,
    halo_send, halo_recv, weight_send, weight_recv,
    reduced, part_send, part_recv, zsum_recv, update_recv, square_recv, own_update,
    rest, halo_top, part_top, zsum_top, update_top,
    local_sem, tile_sem, block_sem, halo_sem, weight_sem, part_sem, zsum_sem, update_sem, square_sem, rest_sem,
):
    me = lax.axis_index("dom")
    z, q = me // NQ, me % NQ
    nxt, prv = (me + 1) % NDEV, (me + NDEV - 1) % NDEV

    load_basis = pltpu.make_async_copy(basis_hbm, basis, local_sem.at[0])
    load_ext = pltpu.make_async_copy(ext_hbm, ext, local_sem.at[1])
    load_basis.start()
    load_ext.start()

    def in_plane(j):
        return z * NQ + (q + j) % NQ

    def in_column(j):
        return ((z + j) % NZ) * NQ + q

    barrier = pltpu.get_barrier_semaphore()

    def greet_plane(j, c):
        pl.semaphore_signal(barrier, inc=1, device_id=(in_plane(j),), device_id_type=MESH)
        return c

    def greet_column(j, c):
        pl.semaphore_signal(barrier, inc=1, device_id=(in_column(j),), device_id_type=MESH)
        return c

    lax.fori_loop(1, NQ, greet_plane, 0)
    lax.fori_loop(1, NZ, greet_column, 0)
    pl.semaphore_signal(barrier, inc=1, device_id=(nxt,), device_id_type=MESH)
    pl.semaphore_signal(barrier, inc=1, device_id=(prv,), device_id_type=MESH)

    tiles[z, 0:4, :] = coef_ref[...]
    row4 = iota((4, C), 0)
    pre = jnp.zeros((4, C), F32)
    for k in range(4):
        pre = jnp.where(row4 == k, precond_ref[k], pre)
    tiles[z, 4:8, :] = pre

    pl.semaphore_wait(barrier, NQ - 1 + NZ - 1 + 2)

    pending = []

    def send_column(src, buf, sems):
        pending.append((buf, NZ - 1, sems.at[0]))

        def body(j, c):
            pltpu.make_async_remote_copy(
                src, buf.at[z], sems.at[0], sems.at[1], device_id=(in_column(j),), device_id_type=MESH
            ).start()
            return c

        lax.fori_loop(1, NZ, body, 0)

    def send_plane(src_of, buf, sems):
        pending.append((buf, NQ - 1, sems.at[0]))

        def body(j, c):
            pltpu.make_async_remote_copy(
                src_of((q + j) % NQ), buf.at[q], sems.at[0], sems.at[1], device_id=(in_plane(j),), device_id_type=MESH
            ).start()
            return c

        lax.fori_loop(1, NQ, body, 0)

    def wait_for(buf, count, sem):
        part = buf.at[pl.ds(0, count)]
        pltpu.make_async_copy(part, part, sem).wait()

    send_column(tiles.at[z], tiles, tile_sem)

    conn[...] = jnp.full(conn.shape, -1.0, F32)
    conn[0:8, 0:ELEMS] = conn_ref[...].astype(F32)
    conn[8:9, 0:ELEMS] = plastic_ref[...].astype(F32)
    halo_row = halo_ref[...].astype(F32)

    def decode(c, carry):
        at = pl.multiple_of(c * 32, 32)
        rows = pl.ds(at, 32)
        place = (iota((32, 512), 0) + (at + 512)).astype(F32)
        found = jnp.full((32, 512), -1.0, F32)
        for a in range(4):
            found = jnp.maximum(found, jnp.where(conn[4 + a : 5 + a, :] == place, conn[a : a + 1, :], -1.0))
        node1 = jnp.max(found, axis=1, keepdims=True)
        mine = iota((32, LAYER), 0) + at == iota((32, LAYER), 1)
        node0 = jnp.sum(jnp.where(mine, halo_row, 0.0), axis=1, keepdims=True)
        flags = conn[8:9, :]
        flag1 = jnp.sum(jnp.where(conn[0:1, :] == node0, flags, 0.0), axis=1, keepdims=True)
        flag2 = jnp.sum(jnp.where(conn[4:5, :] == place, flags, 0.0), axis=1, keepdims=True)
        cell = iota((32, C), 0) + at
        valid = (cell % 16 < 15) & (cell // 16 < 15)
        weight[1, rows, :] = jnp.where(valid, 1.0 + flag1, 0.0)
        second = jnp.where(valid, 1.0 + flag2, 0.0)
        weight[2, rows, :] = second
        weight_send[rows, :] = second.astype(BF16)
        nodes[rows, :] = jnp.broadcast_to(node0 * 3.0, (32, C)).astype(jnp.int32)
        nodes[pl.ds(pl.multiple_of(LAYER + c * 32, 32), 32), :] = jnp.broadcast_to(node1 * 3.0, (32, C)).astype(jnp.int32)
        return carry

    lax.fori_loop(0, LAYER // 32, decode, 0)

    to_next = pltpu.make_async_remote_copy(
        weight_send, weight_recv, weight_sem.at[0], weight_sem.at[1], device_id=(nxt,), device_id_type=MESH
    )
    to_next.start()

    lane = iota((16, C), 1)

    def select(c, carry):
        node3 = nodes[pl.ds(pl.multiple_of(c * 16, 16), 16), :]
        for i in range(3):
            rows = pl.ds(pl.multiple_of((c // 16 * 3 + i) * LAYER + c % 16 * 16, 16), 16)
            away = node3 + i - lane
            for t in range(ROWS // C):
                sel[rows, C * t : C * t + C] = jnp.where(away == C * t, 1.0, 0.0).astype(BF16)
        return carry

    lax.fori_loop(0, 32, select, 0)

    wait_for(tiles, NZ - 1, tile_sem.at[1])
    low = low_half((8, C))
    for j in range(4):
        a, b = tiles[2 * j], tiles[2 * j + 1]
        block_init[8 * j : 8 * j + 8, :] = jnp.where(low, a, swap4(b))
        precond32[8 * j : 8 * j + 8, :] = jnp.where(low, swap4(a), b)
    first = block_init[...].astype(BF16)
    gathered[q] = first
    send_plane(lambda _: gathered.at[q], gathered, block_sem)
    rest[q] = (block_init[...] - first.astype(F32)).astype(BF16)
    send_plane(lambda _: rest.at[q], rest, rest_sem)

    load_basis.wait()

    def permute(c, carry):
        rows = pl.ds(pl.multiple_of(c * 768, 768), 768)
        grid_basis[rows, :] = dot(sel[rows, :], basis[...]).astype(BF16)
        return carry

    lax.fori_loop(0, 2, permute, 0)

    def scales(c, carry):
        node3 = nodes[pl.ds(pl.multiple_of(c * 16, 16), 16), :]
        for i in range(3):
            tile = (node3 + i) >> 7
            value = jnp.zeros((16, C), F32)
            for t in range(12):
                value = jnp.where(tile == t, scale_ref[t], value)
            scale[pl.ds(pl.multiple_of((c // 16 * 3 + i) * LAYER + c % 16 * 16, 16), 16), :] = value
        return carry

    lax.fori_loop(0, 32, scales, 0)

    zero_rows = jnp.zeros((16, C), F32)
    for k in range(12):
        disp[k, LAYER : LAYER + 16, :] = zero_rows
    for k in range(6):
        resid[k, LAYER : LAYER + 16, :] = zero_rows

    def place_rows(values):
        v = values.reshape(16, 2, 4, 8, C)
        first, second = v[:, 0], v[:, 1]
        mask = low_half((16, 4, 8, C))
        even = jnp.where(mask, first, swap4(second))
        odd = jnp.where(mask, swap4(first), second)
        for j in range(4):
            coef_low[256 * j : 256 * j + 128, :] = even[:, j].reshape(128, C).astype(BF16)
            coef_low[256 * j + 128 : 256 * j + 256, :] = odd[:, j].reshape(128, C).astype(BF16)

    wait_for(gathered, NQ - 1, block_sem.at[1])
    place_rows(gathered[...].astype(F32))

    def elements(k):
        def body(c, carry):
            at = pl.multiple_of(c * CHUNK, CHUNK)
            node_rows = pl.ds(at, CHUNK + 16)
            n = CHUNK + 16
            grad = []
            for i in range(3):
                under, over = disp[3 * k + i, node_rows, :], disp[3 * k + 3 + i, node_rows, :]
                under1, over1 = pltpu.roll(under, n - 1, 0), pltpu.roll(over, n - 1, 0)
                both, both1 = under + over, under1 + over1
                dx = both1 - both
                sx = both1 + both
                sz = (over1 + over) - (under1 + under)
                grad.append((dx[16:] + dx[:CHUNK], sx[16:] - sx[:CHUNK], sz[16:] + sz[:CHUNK]))
            w = weight[k, pl.ds(at, CHUNK), :]
            third = (grad[0][0] + grad[1][1] + grad[2][2]) * (1.0 / 6.0)
            sxx = grad[0][0] * 0.5 - third
            syy = grad[1][1] * 0.5 - third
            szz = grad[2][2] * 0.5 - third
            sxy = (grad[0][1] + grad[1][0]) * 0.25
            sxz = (grad[0][2] + grad[2][0]) * 0.25
            syz = (grad[1][2] + grad[2][1]) * 0.25
            mag2 = sxx * sxx + syy * syy + szz * szz + 2.0 * (sxy * sxy + sxz * sxz + syz * syz)
            plastic = 0.05 + 0.6 * lax.rsqrt(jnp.maximum(mag2, 9.0))
            factor = jnp.where(w > 1.5, plastic, jnp.where(w > 0.5, 0.25, 0.0))
            vol = jnp.where(w > 0.5, third * 0.5625, 0.0)
            stress = {
                (0, 0): vol + factor * sxx, (1, 1): vol + factor * syy, (2, 2): vol + factor * szz,
                (0, 1): factor * sxy, (0, 2): factor * sxz, (1, 2): factor * syz,
            }
            back = {ij: pltpu.roll(s, 1, 0) for ij, s in stress.items()}
            pad = jnp.zeros((16, C), F32)
            for i in range(3):
                ix, iy, iz = (0, i), (min(i, 1), max(i, 1)), (i, 2)
                dx = back[ix] - stress[ix]
                sy = back[iy] + stress[iy]
                sz = back[iz] + stress[iz]
                near, far = dx - sy, dx + sy
                if k >= 1:
                    rows = (3 * (k - 1) + i, node_rows, slice(None))
                    resid[rows] -= jnp.concatenate([near - sz, pad], 0) + jnp.concatenate([pad, far - sz], 0)
                if k <= 1:
                    rows = (3 * k + i, node_rows, slice(None))
                    resid[rows] -= jnp.concatenate([near + sz, pad], 0) + jnp.concatenate([pad, far + sz], 0)
            return carry

        lax.fori_loop(0, LAYER // CHUNK, body, 0)

    sent_pieces = []
    for sweep in range(2):
        pieces = ([], [])
        for i in range(3):
            for layer, (there, side) in enumerate(((prv, 1), (nxt, 0))):
                rows = slice((3 * layer + i) * LAYER, (3 * layer + i + 1) * LAYER)
                u = dot(grid_basis[rows, :], coef_low[...]) * scale[rows, :]
                disp[3 + 3 * layer + i, 0:LAYER, :] = u
                top = peak(u)
                halo_top[sweep, layer, i] = top
                halo_send[sweep, layer, i] = to_steps(u, top)
                for src, dst, kind in (
                    (halo_send.at[sweep, layer, i], halo_recv.at[sweep, side, i], 0),
                    (halo_top.at[sweep, layer, i], halo_top.at[sweep, 2 + side, i], 1),
                ):
                    sems = halo_sem.at[sweep, 6 * layer + 2 * i + kind]
                    copy = pltpu.make_async_remote_copy(
                        src, dst, sems.at[0], sems.at[1], device_id=(there,), device_id_type=MESH
                    )
                    copy.start()
                    pieces[layer].append(copy)

        if sweep == 0:
            load_ext.wait()
            ext3 = split3(ext[...])

            def permute_ext(c, carry):
                rows = pl.ds(pl.multiple_of(c * LAYER, LAYER), LAYER)
                e = dot(sel[rows, :], ext3)
                grid_ext[c] = e[:, 0:C] + e[:, C : 2 * C] + e[:, 2 * C :]
                return carry

            lax.fori_loop(0, 6, permute_ext, 0)

            def turn(c, carry):
                rows = pl.ds(pl.multiple_of(c * LAYER, LAYER), LAYER)
                for b in range(4):
                    grid_basis_t[b * 256 : b * 256 + 256, rows] = grid_basis[rows, b * 256 : b * 256 + 256].T
                return carry

            lax.fori_loop(0, 6, turn, 0)
            to_next.wait()
            weight[0] = jnp.where(me > 0, weight_recv[...].astype(F32), 0.0)

        resid[:, 0:LAYER, :] = grid_ext[...]
        elements(1)
        for layer, side in ((0, 1), (1, 0)):
            for copy in pieces[layer]:
                copy.wait_recv()
            for i in range(3):
                u = from_steps(halo_recv[sweep, side, i], halo_top[sweep, 2 + side, i])
                disp[9 * side + i, 0:LAYER, :] = jnp.where(me < NDEV - 1, u, 0.0) if side == 1 else u
            elements(2 * side)
        sent_pieces += pieces[0] + pieces[1]
        for k in range(6):
            rows = slice(k * LAYER, (k + 1) * LAYER)
            scaled[rows, :] = (resid[k, 0:LAYER, :] * scale[rows, :]).astype(BF16)

        mask = low_half((16, 8, C))
        for j in range(4):
            r = dot(grid_basis_t[256 * j : 256 * j + 256, :], scaled[...]).reshape(2, 16, 8, C)
            even, odd = r[0], r[1]
            reduced[:, 0, 8 * j : 8 * j + 8, :] = jnp.where(mask, even, swap4(odd))
            reduced[:, 1, 8 * j : 8 * j + 8, :] = jnp.where(mask, swap4(even), odd)
        parts = reduced[...].reshape(NQ, BLOCK, C)
        top = peak(parts)
        part_top[sweep, q] = top
        part_send[sweep] = to_steps(parts, top[None])
        part_recv[sweep, q] = part_send[sweep, q]
        send_plane(lambda t: part_send.at[sweep, t], part_recv.at[sweep], part_sem.at[sweep, 0])
        send_plane(lambda _: part_top.at[sweep, q], part_top.at[sweep], part_sem.at[sweep, 1])

        if sweep == 1:
            out_local[...] = jnp.zeros_like(out_local)

            def restore(c, carry):
                rows = pl.ds(pl.multiple_of(c * LAYER, LAYER), LAYER)
                o = lax.dot_general(
                    sel[rows, :], split3(resid[c, 0:LAYER, :]), (((0,), (0,)), ((), ())), preferred_element_type=F32
                )
                out_local[...] += o[:, 0:C] + o[:, C : 2 * C] + o[:, 2 * C :]
                return carry

            lax.fori_loop(0, 6, restore, 0)

        wait_for(part_recv.at[sweep], NQ - 1, part_sem.at[sweep, 0, 1])
        wait_for(part_top.at[sweep], NQ - 1, part_sem.at[sweep, 1, 1])
        total = from_steps(part_recv[sweep, 0], part_top[sweep, 0])
        for t in range(1, NQ):
            total += from_steps(part_recv[sweep, t], part_top[sweep, t])
        top = peak(total)
        zsum_top[sweep, z] = top
        zsum_recv[sweep, z] = to_steps(total, top)
        send_column(zsum_recv.at[sweep, z], zsum_recv.at[sweep], zsum_sem.at[sweep, 0])
        send_column(zsum_top.at[sweep, z], zsum_top.at[sweep], zsum_sem.at[sweep, 1])
        wait_for(zsum_top.at[sweep], NZ - 1, zsum_sem.at[sweep, 1, 1])
        wait_for(zsum_recv.at[sweep], NZ - 1, zsum_sem.at[sweep, 0, 1])
        total = from_steps(zsum_recv[sweep, 0], zsum_top[sweep, 0])
        for t in range(1, NZ):
            total += from_steps(zsum_recv[sweep, t], zsum_top[sweep, t])
        update = total * precond32[...]

        if sweep == 0:
            own_update[...] = update
            top = peak(update)
            update_top[q] = top
            update_recv[q] = to_steps(update, top)
            send_plane(lambda _: update_recv.at[q], update_recv, update_sem.at[0])
            send_plane(lambda _: update_top.at[q], update_top, update_sem.at[1])
            wait_for(rest, NQ - 1, rest_sem.at[1])
            gathered0[...] = gathered[...].astype(F32) + rest[...].astype(F32)
            wait_for(update_top, NQ - 1, update_sem.at[1, 1])
            wait_for(update_recv, NQ - 1, update_sem.at[0, 1])
            u = from_steps(update_recv[...], update_top[...])
            squares = jnp.sum(u * u, axis=(0, 1), keepdims=False)[None, :]
            inverse = STEP_SIZE * lax.rsqrt(squares * (1.0 / R) + EPSILON)
            place_rows(gathered0[...] + u * inverse[None])
            block_init[...] += own_update[...] * inverse
        else:
            square_recv[q] = jnp.sum(update * update, axis=0, keepdims=True)
            send_plane(lambda _: square_recv.at[q], square_recv, square_sem)
            wait_for(square_recv, NQ - 1, square_sem.at[1])
            squares = jnp.sum(square_recv[...], axis=0)
            inverse = STEP_SIZE * lax.rsqrt(squares * (1.0 / R) + EPSILON)
            final = block_init[...] + update * inverse
            mine = jnp.zeros((8, C), F32)
            for j in range(4):
                mine = jnp.where(z // 2 == j, final[8 * j : 8 * j + 8], mine)
            mine = jnp.where(z % 2 == 0, mine, swap4(mine))
            final_ref[...] = mine[0:4]

    for copy in sent_pieces:
        copy.wait_send()
    for sent in pending:
        wait_for(*sent)


def on_device(coef_init, basis, basis_scale, ext_force, precond, connectivity, halo_nodes, plastic):
    vmem = pl.BlockSpec(memory_space=pltpu.VMEM)
    smem = pl.BlockSpec(memory_space=pltpu.SMEM)
    anywhere = pl.BlockSpec(memory_space=pl.ANY)
    dma = pltpu.SemaphoreType.DMA
    return pl.pallas_call(
        kernel,
        out_shape=(pltpu.VMEM((4, C), F32), pltpu.VMEM((ROWS, C), F32)),
        in_specs=[vmem, smem, smem, vmem, vmem, vmem, anywhere, anywhere],
        out_specs=(vmem, vmem),
        scratch_shapes=[
            pltpu.VMEM((ROWS, R), BF16),
            pltpu.VMEM((ROWS, C), F32),
            pltpu.VMEM((ROWS, ROWS), BF16),
            pltpu.VMEM((ROWS, R), BF16),
            pltpu.VMEM((R, ROWS), BF16),
            pltpu.VMEM((ROWS, C), F32),
            pltpu.VMEM((6, LAYER, C), F32),
            pltpu.VMEM((6, LAYER + 16, C), F32),
            pltpu.VMEM((12, LAYER + 16, C), F32),
            pltpu.VMEM((3, LAYER, C), F32),
            pltpu.VMEM((16, 512), F32),
            pltpu.VMEM((2 * LAYER, C), jnp.int32),
            pltpu.VMEM((NZ, 8, C), F32),
            pltpu.VMEM((BLOCK, C), F32),
            pltpu.VMEM((BLOCK, C), F32),
            pltpu.VMEM((NQ, BLOCK, C), BF16),
            pltpu.VMEM((NQ, BLOCK, C), F32),
            pltpu.VMEM((R, C), BF16),
            pltpu.VMEM((ROWS, C), BF16),
            pltpu.VMEM((2, 2, 3, LAYER, C), jnp.int16),
            pltpu.VMEM((2, 2, 3, LAYER, C), jnp.int16),
            pltpu.VMEM((LAYER, C), BF16),
            pltpu.VMEM((LAYER, C), BF16),
            pltpu.VMEM((16, 2, BLOCK, C), F32),
            pltpu.VMEM((2, NQ, BLOCK, C), jnp.int16),
            pltpu.VMEM((2, NQ, BLOCK, C), jnp.int16),
            pltpu.VMEM((2, NZ, BLOCK, C), jnp.int16),
            pltpu.VMEM((NQ, BLOCK, C), jnp.int16),
            pltpu.VMEM((NQ, 1, C), F32),
            pltpu.VMEM((BLOCK, C), F32),
            pltpu.VMEM((NQ, BLOCK, C), BF16),
            pltpu.VMEM((2, 4, 3, 1, C), F32),
            pltpu.VMEM((2, NQ, 1, C), F32),
            pltpu.VMEM((2, NZ, 1, C), F32),
            pltpu.VMEM((NQ, 1, C), F32),
            dma((2,)),
            dma((2,)),
            dma((2,)),
            dma((2, 12, 2)),
            dma((2,)),
            dma((2, 2, 2)),
            dma((2, 2, 2)),
            dma((2, 2)),
            dma((2,)),
            dma((2,)),
        ],
        compiler_params=pltpu.CompilerParams(
            collective_id=0, has_side_effects=True, vmem_limit_bytes=58 << 20
        ),
        cost_estimate=pl.CostEstimate(flops=14_000_000_000, bytes_accessed=6_000_000, transcendentals=0),
        name="galerkin",
    )(
        coef_init, basis_scale, precond, connectivity.T, halo_nodes.reshape(1, LAYER), plastic.reshape(1, ELEMS),
        basis, ext_force,
    )


def solution(mesh):
    return jax.shard_map(
        on_device,
        mesh=mesh,
        in_specs=(
            P("dom", None), P("dom", None), P("dom"), P("dom", None), P("dom"), P("dom", None), P("dom"), P("dom"),
        ),
        out_specs=(P("dom", None), P("dom", None)),
        check_vma=False,
    )
```
